512 devices in a mesh: img: 8 (over x, core), vol: 64 (over z, y).
Axes of the slice: x: 4, y: 8, z: 8, core: 2. Of those that a mesh axis runs over, the one named last changes fastest.
Arguments:
- density: float32 [256, 256, 256], P('vol', 'img'), may hold values from -6 to 6
- images: bfloat16 [4096, 2, 128, 256], P(('img', 'vol')), may hold values from -6 to 6
- block_tiles: int32 [2048, 128], P('img'), may hold values from 0 to 65535, as said below
- image_blocks: int32 [4096, 2], P(('img', 'vol')), may hold values from 0 to 3, all different within a row
- shifts: int32 [4096, 16], P(('img', 'vol')), may hold values from -8 to 8
- precision: float32 [4096], P(('img', 'vol')), may hold values from 0.002 to 0.02
Outputs:
- updated_map: float32 [256, 256, 2, 256], P('vol', 'img')
- posterior: float32 [4096, 2, 16], P(('img', 'vol'))
The draws below stay inside these ranges and needn't reach their ends.
Inputs may be any that keep to these rules, and one draw needn't show every extreme that they name: `block_tiles`: entry q * 256 + p names the tile at (q, p). Row r of a block names p = 2 r or 2 r + 1, one of the two for the whole block. Among the entries of the 4 blocks of one device at most 16 have q in one slab of 4 values (q // 4 equal), and some device reaches 16 in every draw. `image_blocks`: each row names 2 different blocks.
All inputs are finite; a program needn't handle non-finite values.
Results may differ from the reference program's by a relative error of at most 0.005.
Values may be sent and summed in bfloat16 or wider, within the bound.
No kernel may reach another device: no remote copies, remote signals or barrier semaphores. Data moves between devices by JAX's collectives and lax.ppermute only.
A program may use at most 64 MiB of HBM per device.

```python
import math
import jax
import jax.numpy as jnp
from jax import lax

BOX = 256
SLICE_ROWS = 128
TRANS = 16
CHOSEN = 2
SLOPE_MAX = 4
BLOCKS_DEV = 4
IMG_DEV = 8
SLAB = 4
IMAGES = 4096
N_IMG = 8
N_VOL = 64


def draw_block_tiles(key, part):
    key = jax.random.fold_in(key, 11)
    keys = jax.random.split(key, 5)
    nblocks = BLOCKS_DEV * N_IMG * N_VOL
    slope_pick = jax.random.randint(keys[0], (nblocks,), 0, 3)
    slopes = jnp.maximum(SLOPE_MAX // 2 ** slope_pick, 1)
    start_owner = jax.random.randint(keys[1], (nblocks,), 0, N_VOL)
    offset_q = jax.random.randint(keys[2], (nblocks,), 0, SLAB)
    parity = jax.random.randint(keys[3], (nblocks,), 0, 2)
    forced = jax.random.randint(keys[4], (), 0, N_IMG * N_VOL)
    device_of = jnp.arange(nblocks) // BLOCKS_DEV
    hit = device_of == forced
    slopes = jnp.where(hit, SLOPE_MAX, slopes)
    offset_q = jnp.where(hit, 0, offset_q)
    start_owner = jnp.where(hit, start_owner[forced * BLOCKS_DEV], start_owner)
    row_index = jnp.arange(SLICE_ROWS)
    q_value = jnp.mod(start_owner[:, None] * SLAB + offset_q[:, None] + SLAB * row_index[None, :] // slopes[:, None], BOX)
    p_value = jnp.mod(2 * row_index[None, :] + parity[:, None], BOX)
    return (q_value * BOX + p_value).astype(jnp.int32)


def place_ends(values, own_key, least, high):
    longest = values.shape.index(max(values.shape))
    spots = []
    for shift in (0, 1):
        where = [jax.random.randint(jax.random.fold_in(own_key, axis), (), 0, length) for axis, length in enumerate(values.shape)]
        where[longest] = (where[longest] + shift) % values.shape[longest]
        spots.append(tuple(where))
    return values.at[spots[0]].set(least).at[spots[1]].set(high)


def shard_levels(key, dims, shards, low, top_value):
    def one(dim, blocks):
        steps = jax.random.uniform(jax.random.fold_in(jax.random.fold_in(key, 6), dim), (blocks,), jnp.float32, low / len(shards), top_value / len(shards))
        return jnp.repeat(jnp.exp(steps), dims[dim] // blocks).reshape((-1,) + (1,) * (len(dims) - dim - 1))

    gain = one(*shards[0])
    for cut in shards[1:]:
        gain = gain * one(*cut)
    return gain


def distinct(rng, rows, number_of, top, lift):
    ranking = jax.random.permutation(jax.random.fold_in(rng, 1), number_of)
    boost = ranking
    for power in range(3):
        boost = boost * boost // number_of
    boost = boost * lift // number_of
    lots = jax.random.randint(jax.random.fold_in(rng, 2), (rows, number_of), 0, 4096) + boost
    sure = jax.random.permutation(jax.random.fold_in(rng, 3), rows)[jnp.arange(number_of) % rows]
    lots = jnp.where(jnp.arange(rows)[:, None] == sure[None, :], 1 << 14, lots)
    merit = lots * number_of + jnp.arange(number_of)
    return lax.top_k(merit.astype(jnp.int32), top)[1].astype(jnp.int32)


def scatter_about(stream_key, extent, deviation, most, pieces=(), dtype=jnp.bfloat16):
    entries = deviation * jax.random.normal(stream_key, extent, jnp.float32)
    if pieces:
        entries = entries * shard_levels(stream_key, extent, pieces, -0.22, 0.18)
    return jnp.clip(entries, -most, most).astype(dtype)


def setup_inputs(seed: int = 0) -> dict:
    seeds = jax.random.split(jax.random.key(seed), 7)
    density = scatter_about(seeds[0], (BOX, BOX, BOX), 1.0, 6.0, ((0, 64), (1, 8)), jnp.float32)
    images = scatter_about(seeds[1], (IMAGES, 2, SLICE_ROWS, BOX), 1.0, 6.0, ((0, 512),))
    block_tiles = draw_block_tiles(jax.random.fold_in(seeds[6], 71), 0)
    image_blocks = distinct(seeds[3], IMAGES, BLOCKS_DEV, CHOSEN, 8192)
    shifts = place_ends(jax.random.randint(seeds[4], (IMAGES, TRANS), -8, 9), jax.random.fold_in(seeds[4], 1), -8, 8).astype(jnp.int32)
    precision = jnp.clip(jnp.exp(math.log(0.02) - 2.30258502 * jax.random.uniform(seeds[5], (IMAGES,), jnp.float32) ** shard_levels(seeds[5], (IMAGES,), ((0, 512),), -0.2, 0.2)), 0.002, 0.02)
    return {"density": density, "images": images, "block_tiles": block_tiles, "image_blocks": image_blocks, "shifts": shifts, "precision": precision}


HIGH = lax.Precision.HIGHEST


def score_blocks(image_set, slices, chosen, offsets, row_precision):
    count = image_set.shape[0]
    image_wide = image_set.astype(jnp.float32)
    slice_wide = slices.astype(jnp.float32)
    products = jnp.einsum("icrf,brdf->ibcdf", image_wide, slice_wide, precision=HIGH)
    corr_re = products[:, :, 0, 0] + products[:, :, 1, 1]
    corr_im = products[:, :, 1, 0] - products[:, :, 0, 1]
    energy = jnp.sum(jnp.square(slice_wide), axis=(1, 2, 3))
    picked = (chosen[:, :, None] == jnp.arange(BLOCKS_DEV)[None, None, :]).astype(jnp.float32)
    sel_re = jnp.sum(picked[:, :, :, None] * corr_re[:, None], axis=2)
    sel_im = jnp.sum(picked[:, :, :, None] * corr_im[:, None], axis=2)
    sel_energy = jnp.sum(picked * energy[None, None, :], axis=2)
    frequency = jnp.arange(BOX)
    turns = jnp.mod(offsets[:, :, None] * frequency[None, None, :], BOX).astype(jnp.float32)
    phases = turns * (2.0 * math.pi / BOX)
    cos_shift = jnp.cos(phases)
    sin_shift = jnp.sin(phases)
    match_score = jnp.einsum("ilf,itf->ilt", sel_re, cos_shift, precision=HIGH) + jnp.einsum("ilf,itf->ilt", sel_im, sin_shift, precision=HIGH)
    logits = row_precision[:, None, None] * (match_score - 0.5 * sel_energy[:, :, None])
    weights = jax.nn.softmax(logits.reshape(count, -1), axis=1).reshape(logits.shape)
    back_re = jnp.einsum("ilt,itf->ilf", weights, cos_shift, precision=HIGH)
    back_im = -jnp.einsum("ilt,itf->ilf", weights, sin_shift, precision=HIGH)
    block_re = jnp.sum(picked[:, :, :, None] * back_re[:, :, None], axis=1)
    block_im = jnp.sum(picked[:, :, :, None] * back_im[:, :, None], axis=1)
    factor = jnp.stack([block_re, block_im], axis=2).astype(jnp.bfloat16)
    spread = jnp.einsum("icrf,ibdf->brcdf", image_wide, factor.astype(jnp.float32), precision=HIGH)
    rows_re = spread[:, :, 0, 0] - spread[:, :, 1, 1]
    rows_im = spread[:, :, 0, 1] + spread[:, :, 1, 0]
    back_rows = jnp.stack([rows_re, rows_im], axis=2)
    block_mass = jnp.sum(picked * jnp.sum(weights, axis=2)[:, :, None], axis=(0, 1))
    return weights, back_rows, block_mass


def reference(density, images, block_tiles, image_blocks, shifts, precision):
    spectrum = jnp.fft.fftn(density) / (BOX ** 1.5)
    planes = jnp.stack([jnp.real(spectrum), jnp.imag(spectrum)], axis=0)
    fourier = jnp.transpose(planes, (2, 1, 0, 3))
    tile_rows = fourier.reshape(BOX * BOX, 2, BOX)
    tile_half = tile_rows.astype(jnp.bfloat16)
    groups = N_IMG * N_VOL
    device_parts = (
        images.reshape(groups, IMG_DEV, 2, SLICE_ROWS, BOX),
        block_tiles.reshape(groups, BLOCKS_DEV * SLICE_ROWS),
        image_blocks.reshape(groups, IMG_DEV, CHOSEN),
        shifts.reshape(groups, IMG_DEV, TRANS),
        precision.reshape(groups, IMG_DEV),
    )

    def one_device(parts_now):
        image_set, tile_list, chosen, offsets, row_precision = parts_now
        slices = jnp.take(tile_half, tile_list.astype(jnp.int32), axis=0).reshape(BLOCKS_DEV, SLICE_ROWS, 2, BOX)
        return score_blocks(image_set, slices, chosen, offsets, row_precision)

    weights, back_rows, block_mass = lax.map(one_device, device_parts)
    flat_tiles = block_tiles.reshape(-1).astype(jnp.int32)
    totals = jnp.zeros((BOX * BOX, 2, BOX), jnp.float32).at[flat_tiles].add(back_rows.reshape(-1, 2, BOX))
    masses = jnp.zeros((BOX * BOX,), jnp.float32).at[flat_tiles].add(jnp.repeat(block_mass.reshape(-1), SLICE_ROWS))
    updated = (totals + tile_rows) / (1.0 + masses)[:, None, None]
    return updated.reshape(BOX, BOX, 2, BOX), weights.reshape(IMAGES, CHOSEN, TRANS)
```

```python
import functools
import math

import jax
import jax.numpy as jnp
import numpy as np
from jax import lax
from jax.experimental import pallas as pl
from jax.experimental.pallas import tpu as pltpu
from jax.sharding import PartitionSpec as P

N = 256
NG = 8
NV = 64
SLAB = 4
NB = 4
ROWS = 128
CAP = 16
FJ = N // NG
TR = 16
F32 = jnp.float32
BF = jnp.bfloat16
HI = lax.Precision.HIGHEST
VM = 100 * 1024 * 1024 // 2


def dot32(a, b):
    return jnp.dot(a, b, precision=HI, preferred_element_type=F32)


def dot16(a, b):
    return jnp.dot(a, b, preferred_element_type=F32)


def dot_nt(a, b, precision=None):
    return lax.dot_general(
        a, b, (((1,), (1,)), ((), ())), precision=precision, preferred_element_type=F32
    )


def lanes(shape):
    return lax.broadcasted_iota(jnp.int32, shape, len(shape) - 1)


def swap4(parts):
    group = lanes(parts[0].shape) // 32
    out = []
    for b in range(4):
        acc = None
        for a in range(4):
            shift = (32 * (a - b)) % 128
            moved = parts[a] if shift == 0 else pltpu.roll(parts[a], shift, 1)
            acc = moved if acc is None else jnp.where(group == a, moved, acc)
        out.append(acc)
    return out


def table_first():
    n = np.arange(N)
    ang = 2.0 * np.pi * ((n[:, None] * n[None, :]) % N) / N
    return np.concatenate([np.cos(ang), -np.sin(ang)], axis=1).astype(np.float32)


def table_second():
    k = np.arange(N).reshape(NV, SLAB)
    n = np.arange(N)
    ang = 2.0 * np.pi * ((k[:, :, None] * n[None, None, :]) % N) / N
    c, s = np.cos(ang), np.sin(ang)
    left = np.stack([c, -s], axis=1).reshape(2 * N, N)
    right = np.stack([s, c], axis=1).reshape(2 * N, N)
    return np.stack([left, right]).astype(np.float32)


def table_third():
    k = np.arange(N)
    n = (np.arange(NV)[None, :] * 4 + np.arange(4)[:, None]).reshape(-1)
    ang = 2.0 * np.pi * ((k[:, None] * n[None, :]) % N) / N
    scale = float(N) ** -1.5
    return np.stack([np.cos(ang) * scale, np.sin(ang) * scale]).astype(np.float32)


def table_fold():
    out = np.zeros((2, 4, 32, 2, 2, 32), np.float32)
    for c in range(2):
        for j in range(32):
            out[c, :, j, :, c, j] = 1.0
    return out.reshape(256, 128)


def table_spread():
    out = np.zeros((2, 2, 2, 32, 2, 4, 32), np.float32)
    for h in range(2):
        for c in range(2):
            for j in range(32):
                out[h, h, c, j, c, :, j] = 1.0
    return out.reshape(2, 128, 256)


def fill_lists(at_ref, tiles_ref, params_ref, o_ref):
    tiles = jnp.concatenate([tiles_ref[:, b, :] for b in range(NB)], axis=1)
    at = at_ref[0]
    width = NB * ROWS
    lane = lanes((NV, width))
    sub = lax.broadcasted_iota(jnp.int32, (NV, width), 0)
    earlier = jnp.where(
        lax.broadcasted_iota(jnp.int32, (width, width), 0) < lanes((width, width)), 1.0, 0.0
    ).astype(BF)

    owned = jnp.right_shift(tiles, 10) == at
    rank = dot16(jnp.where(owned, 1.0, 0.0).astype(BF), earlier).astype(jnp.int32)
    coded = jnp.bitwise_and(tiles, 1023) + jnp.right_shift(lane, 7) * 1024 + 1
    rank = jnp.where(owned, rank, -1)
    short = lanes((NV, 128))
    table = jnp.zeros((NV, 128), F32)
    for s in range(CAP):
        code = jnp.sum(jnp.where(rank == s, coded, 0).astype(F32), axis=1, keepdims=True)
        table = jnp.where(short == s, code, table)
    table = jnp.concatenate([table, table], axis=0) - 1.0
    codes = table.T[:CAP]

    mine = jnp.concatenate(
        [tiles_ref[pl.ds(at, 1), b, :] for b in range(NB)], axis=1
    )
    owner = jnp.right_shift(mine, 10)
    hot = sub == owner
    count = dot16(jnp.where(hot, 1.0, 0.0).astype(BF), earlier)
    place = jnp.sum(jnp.where(hot, count, 0.0), axis=0, keepdims=True).astype(jnp.int32)
    pos = owner * CAP + place
    row = lanes((8, width))
    kind = lax.broadcasted_iota(jnp.int32, (8, width), 0)
    digits = jnp.where(
        kind == 0, jnp.right_shift(row, 5), jnp.where(kind == 1, jnp.bitwise_and(row, 31), 1)
    ).astype(F32).astype(BF)
    found = jnp.where(
        lax.broadcasted_iota(jnp.int32, (NV * CAP, width), 0) == pos, 1.0, 0.0
    ).astype(BF)
    read = dot_nt(digits, found)
    inv = read[0:1] * 32.0 + read[1:2] + read[2:3] - 1.0
    pos = pos.astype(F32)
    params = params_ref[...]
    for k in range(NG):
        o_ref[k, 64:80] = codes
        for q in range(8):
            o_ref[k, 80 + q : 81 + q] = inv[:, q * 128 : q * 128 + 128]
        for q in range(4):
            o_ref[k, 88 + q : 89 + q] = pos[:, q * 128 : q * 128 + 128]
        o_ref[k, 92:96] = jnp.zeros((4, 128), F32)
        o_ref[k, 96:104] = params


def first_kernel(at_ref, d_ref, t_ref, tiles_ref, params_ref, o_ref):
    table = t_ref[...]
    rows = [dot32(d_ref[n0], table) for n0 in range(4)]
    for c in range(2):
        for hi in range(2):
            at = c * N + hi * 128
            moved = swap4([rows[n0][:, at : at + 128] for n0 in range(4)])
            for lo in range(4):
                o_ref[hi * 4 + lo, c * 32 : c * 32 + 32] = moved[lo]
    fill_lists(at_ref, tiles_ref, params_ref, o_ref)


def second_kernel(x_ref, w_ref, o_ref):
    re = x_ref[:, 0:32].reshape(N, 128)
    im = x_ref[:, 32:64].reshape(N, 128)
    o_ref[...] = (dot32(w_ref[0], re) + dot32(w_ref[1], im)).reshape(NV, 8, 128)


def slot_columns(lists_ref):
    low = lanes((CAP, 128)) < 64
    rows = [
        jnp.where(low, lists_ref[2 * gh, 64:80], lists_ref[2 * gh + 1, 64:80]) for gh in range(4)
    ]
    return jnp.concatenate(rows, axis=0).astype(jnp.int32)


def gather_kernel(x_ref, w_ref, fold_ref, lists_ref, f_ref, o_ref, half):
    parts = []
    for c in range(2):
        moved = swap4([x_ref[:, c * 4 + k, :] for k in range(4)])
        parts.append(jnp.concatenate(moved, axis=0))
    cos_t, sin_t = w_ref[0], w_ref[1]
    f_re = dot32(cos_t, parts[0]) + dot32(sin_t, parts[1])
    f_im = dot32(cos_t, parts[1]) - dot32(sin_t, parts[0])
    f_ref[0] = f_re
    f_ref[1] = f_im
    half[:, :128] = f_re.astype(BF)
    half[:, 128:] = f_im.astype(BF)

    columns = slot_columns(lists_ref)

    def step(nb, carry):
        cols = pltpu.roll(columns, 128 - 4 * nb, 1)
        tile = jnp.concatenate(
            [
                jnp.broadcast_to(cols[:, 64 * h + v : 64 * h + v + 1], (64, 128))
                for v in range(4)
                for h in range(2)
            ],
            axis=0,
        )
        lane = lanes(tile.shape)
        k0 = jnp.bitwise_and(tile, N - 1)
        k1 = jnp.where(tile < 0, -1, jnp.bitwise_and(jnp.right_shift(tile, 8), 3))
        hot = jnp.concatenate(
            [jnp.where(k0 == lane, 1.0, 0.0), jnp.where(k0 == lane + 128, 1.0, 0.0)], axis=1
        ).astype(BF)
        got = dot16(hot, half[...])
        keep = k1 == lane // 32
        kept = jnp.concatenate(
            [jnp.where(keep, got[:, :128], 0.0), jnp.where(keep, got[:, 128:], 0.0)], axis=1
        ).astype(BF)
        packed = dot16(kept, fold_ref[...]).reshape(4, 2, 64, 128)
        low = lanes((4, 64, 128)) < 64
        o_ref[pl.ds(nb * 4, 4)] = jnp.where(low, packed[:, 0], packed[:, 1]).astype(BF)
        return carry

    lax.fori_loop(0, 16, step, 0)


def image_kernel(x_ref, o_ref):
    for hi in range(2):
        parts = [
            x_ref[a // 2, a % 2, :, hi * 128 : hi * 128 + 128].astype(F32) for a in range(4)
        ]
        moved = swap4(parts)
        for lo in range(4):
            o_ref[hi * 4 + lo, 0] = moved[lo].astype(BF)


def score_kernel(x_ref, s_ref, lists_ref, t_ref, o_ref, cp1, cp2, ce):
    gh = pl.program_id(0)
    data = s_ref[...].reshape(NV * CAP, 128)
    half_of = lanes((512, 128)) // 64
    for h in range(2):
        g = gh * 2 + h
        inv = lists_ref[g, 80:88].astype(jnp.int32)
        sub = lax.broadcasted_iota(jnp.int32, (512, 128), 0)
        hot = jnp.concatenate(
            [jnp.where(sub == inv[q : q + 1], 1.0, 0.0).astype(BF) for q in range(8)], axis=1
        )
        got = dot16(hot, data)
        got = jnp.where(half_of == h, got, 0.0)
        rows = got + pltpu.roll(got, 64, 1)
        turned = pltpu.roll(rows, 32, 1)
        for b in range(NB):
            s_a = rows[b * ROWS : (b + 1) * ROWS]
            s_b = turned[b * ROWS : (b + 1) * ROWS]
            energy = jnp.sum(s_a * s_a, axis=0, keepdims=True)
            for ih in range(4):
                image = x_ref[h, ih].astype(F32)
                one = jnp.sum(s_a * image, axis=0, keepdims=True)
                two = jnp.sum(s_b * image, axis=0, keepdims=True)
                for lo in range(2):
                    at = pl.ds(g * 8 + lo * 4 + ih, 1)
                    cp1[b, at, :] = one
                    cp2[b, at, :] = two
                    ce[b, at, :] = energy

    @pl.when(gh == 3)
    def _():
        full = (
            dot32(cp1[...].reshape(256, 128), t_ref[0, 0])
            + dot32(cp2[...].reshape(256, 128), t_ref[0, 1])
            + dot32(ce[...].reshape(256, 128), jnp.full((128, 256), -0.25, F32))
        ).reshape(NB, 64, 256)
        group = lanes((64, 128)) // 32
        first = lax.broadcasted_iota(jnp.int32, (64, 128), 0) % 8 < 4
        table = jnp.zeros((64, 128), F32)
        for b in range(NB):
            own = jnp.where(first, full[b, :, :128], full[b, :, 128:])
            table = jnp.where(group == b, own, table)
        idx = lists_ref[:, 96:104].reshape(64, 128).astype(jnp.int32)
        score = jnp.take_along_axis(table, jnp.bitwise_and(idx, 127), axis=1)
        group = lanes((16, 128)) // 32
        packed = score[:16]
        for q in range(1, 4):
            packed = jnp.where(group == q, pltpu.roll(score[q * 16 : q * 16 + 16], 32 * q, 1), packed)
        for k in range(NG):
            o_ref[k] = packed


def back_kernel(x_ref, p_ref, lists_ref, u_ref, w_ref, o_ref, fr, fi, rows):
    gh = pl.program_id(0)

    @pl.when(gh == 0)
    def _():
        packed = p_ref[0]
        for k in range(1, NG):
            packed = packed + p_ref[k]
        score = jnp.concatenate(
            [packed if q == 0 else pltpu.roll(packed, 128 - 32 * q, 1) for q in range(4)], axis=0
        )
        lane = lanes((64, 128))
        valid = lane < 2 * TR
        params = lists_ref[:, 96:104].reshape(64, 128)
        logits = score * params[:, 32:33]
        top = jnp.max(jnp.where(valid, logits, -jnp.inf), axis=1, keepdims=True)
        expo = jnp.where(valid, jnp.exp(jnp.where(valid, logits - top, 0.0)), 0.0)
        post = expo / jnp.sum(expo, axis=1, keepdims=True)
        w_ref[...] = post
        idx = params.astype(jnp.int32)
        weight = jnp.zeros((64, 128), F32)
        for k in range(2 * TR):
            weight = weight + jnp.where(lane == idx[:, k : k + 1], post[:, k : k + 1], 0.0)
        group = lane // 32
        stacked = jnp.concatenate(
            [jnp.where(group == b, weight, 0.0) for b in range(NB)], axis=0
        )
        fac = dot32(stacked, u_ref[0]).reshape(NB, 64, 256)
        low = lane < 64
        for b in range(NB):
            for part, ref in ((0, fr), (1, fi)):
                val = fac[b, :, part * 128 : part * 128 + 128]
                val = jnp.where(low, val, pltpu.roll(val, 60, 0))
                ref[b] = val.astype(BF).astype(F32)
        block_of = (
            lanes((8, 128)) // 32 == lax.broadcasted_iota(jnp.int32, (8, 128), 0)
        ).astype(F32)
        per_image = dot_nt(block_of, weight, HI)
        sub = lax.broadcasted_iota(jnp.int32, (64, 128), 0)
        per_group = dot32(per_image, (sub // 8 == lane % 32 // 4).astype(F32))
        sub = lax.broadcasted_iota(jnp.int32, (8, 128), 0)
        lane = lanes((8, 128))
        mass = jnp.sum(jnp.where(sub == lane % 4, per_group, 0.0), axis=0, keepdims=True)
        upper = mass.astype(BF).astype(F32)
        middle = (mass - upper).astype(BF).astype(F32)
        piece = lanes((1, 128)) // 32
        mass = jnp.where(
            piece == 0,
            upper,
            jnp.where(piece == 1, middle, jnp.where(piece == 2, mass - upper - middle, 0.0)),
        )
        o_ref[:, 64:72] = jnp.broadcast_to(mass.reshape(1, 1, 128), (NV, 8, 128)).astype(BF)

    low = lanes((NV * CAP, 128)) < 64
    outs = []
    for h in range(2):
        g = gh * 2 + h
        for b in range(NB):
            acc_a = jnp.zeros((ROWS, 128), F32)
            acc_b = jnp.zeros((ROWS, 128), F32)
            for ih in range(4):
                image = x_ref[h, ih].astype(F32)
                at = pl.ds(g * 8 + ih, 1)
                acc_a = acc_a + image * fr[b, at, :]
                acc_b = acc_b + image * fi[b, at, :]
            acc = acc_a + pltpu.roll(acc_a, 64, 1)
            acc_b = acc_b + pltpu.roll(acc_b, 64, 1)
            rows[b * ROWS : (b + 1) * ROWS] = (acc + pltpu.roll(acc_b, 32, 1)).astype(BF)
        pos = lists_ref[g, 88:92].astype(jnp.int32)
        sub = lax.broadcasted_iota(jnp.int32, (NV * CAP, 128), 0)
        hot = jnp.concatenate(
            [jnp.where(sub == pos[q : q + 1], 1.0, 0.0).astype(BF) for q in range(4)], axis=1
        )
        outs.append(dot16(hot, rows[...]))
    at = pl.ds(pl.multiple_of(gh * CAP, CAP), CAP)
    o_ref[:, at, :] = jnp.where(low, outs[0], outs[1]).astype(BF).reshape(NV, CAP, 128)


def total_kernel(x_ref, f_ref, spread_ref, lists_ref, o_ref, tot, msum, codes, slot_mass):
    tot[...] = jnp.zeros_like(tot)
    msum[...] = jnp.zeros_like(msum)
    columns = slot_columns(lists_ref)
    by_slot = jnp.concatenate(
        [lists_ref[2 * gh + h, 64:80] for h in range(2) for gh in range(4)], axis=0
    )
    code = by_slot.T[:NV].astype(jnp.int32)
    codes[...] = code
    sent = x_ref[:, 64:72, :].astype(F32)[:, 0, :]
    source = lax.broadcasted_iota(jnp.int32, (128, 128), 0)
    target = lanes((128, 128))
    group = target % 64 // 16 * 2 + target // 64
    mass = jnp.zeros((NV, 128), F32)
    for b in range(NB):
        pick = (source % 32 == group * 4 + b).astype(F32)
        mass = jnp.where(jnp.right_shift(code, 10) == b, dot32(sent, pick), mass)
    slot_mass[...] = mass

    def step(nb, carry):
        cols = pltpu.roll(columns, 128 - 4 * nb, 1)
        data = x_ref[pl.ds(nb * 4, 4), 0:64, :].reshape(256, 128)
        kept = []
        for h in range(2):
            col = jnp.concatenate(
                [
                    jnp.broadcast_to(cols[:, 64 * h + v : 64 * h + v + 1], (64, 128))
                    for v in range(4)
                ],
                axis=0,
            )
            k1 = jnp.where(col < 0, -1, jnp.bitwise_and(jnp.right_shift(col, 8), 3))
            keep = k1 == lanes((256, 128)) // 32
            wide = dot16(data, spread_ref[h])
            kept.append(
                jnp.concatenate(
                    [jnp.where(keep, wide[:, :128], 0.0), jnp.where(keep, wide[:, 128:], 0.0)],
                    axis=1,
                ).astype(BF)
            )
        kept = jnp.concatenate(
            [kept[h][v * 64 : v * 64 + 64] for v in range(4) for h in range(2)], axis=0
        )
        hots, weights = [], []
        for v in range(4):
            at = pl.ds(nb * 4 + v, 1)
            row = codes[at, :]
            mass = slot_mass[at, :]
            hots.append(
                jnp.where(
                    lax.broadcasted_iota(jnp.int32, (N, 128), 0) == jnp.bitwise_and(row, N - 1),
                    1.0,
                    0.0,
                ).astype(BF)
            )
            sub = lax.broadcasted_iota(jnp.int32, (8, 128), 0)
            hit = (sub % 4 == jnp.bitwise_and(jnp.right_shift(row, 8), 3)) & (row >= 0)
            upper = mass.astype(BF).astype(F32)
            weights.append(
                jnp.where(hit, jnp.where(sub < 4, upper, mass - upper), 0.0).astype(BF)
            )
        hot = jnp.concatenate(hots, axis=1)
        tot[...] += dot16(hot, kept)
        msum[...] += dot_nt(hot, jnp.concatenate(weights, axis=1))
        return carry

    lax.fori_loop(0, 16, step, 0)
    expand = (
        lanes((8, 128)) // 32 == lax.broadcasted_iota(jnp.int32, (8, 128), 0) % 4
    ).astype(F32)
    scale = 1.0 / (1.0 + dot32(msum[...], expand))
    for c in range(2):
        new = (tot[:, c * 128 : c * 128 + 128] + f_ref[c]) * scale
        o_ref[:, c] = new.reshape(NG, FJ, 128)


def last_kernel(x_ref, o_ref):
    for c in range(2):
        for hi in range(2):
            moved = swap4([x_ref[hi * 4 + lo, c] for lo in range(4)])
            for k in range(4):
                o_ref[k, :, c, hi * 128 : hi * 128 + 128] = moved[k]


def call(kernel, out, name, **extra):
    return pl.pallas_call(
        kernel,
        out_shape=out,
        name=name,
        compiler_params=pltpu.CompilerParams(vmem_limit_bytes=VM),
        **extra,
    )


def struct(shape, dtype=F32):
    return jax.ShapeDtypeStruct(shape, dtype)


def over_img(x):
    return lax.all_to_all(x, "img", split_axis=0, concat_axis=0, tiled=True)


def over_vol(x):
    return lax.all_to_all(x, "vol", split_axis=0, concat_axis=0, tiled=True)


def phase_tables():
    freq = np.arange(N).reshape(NG, FJ)
    shift = np.arange(32) - 8
    ang = 2.0 * np.pi * ((freq[:, :, None] * shift[None, None, :]) % N) / N
    cos_t, sin_t = np.cos(ang), np.sin(ang)
    score = np.zeros((NG, 2, 2, 2, FJ, 2, NB, 32), np.float32)
    back = np.zeros((NG, NB, 32, 2, 2, 2, FJ), np.float32)
    for c in range(2):
        sign = 1.0 if c else -1.0
        for lo in range(2):
            score[:, 0, lo, c, :, lo] = cos_t[:, :, None, :]
            score[:, 1, lo, c, :, lo] = sign * sin_t[:, :, None, :]
            back[:, :, :, 0, lo, c, :] = cos_t.transpose(0, 2, 1)[:, None]
            back[:, :, :, 1, lo, c, :] = sign * sin_t.transpose(0, 2, 1)[:, None]
    return score.reshape(NG, 2, 128, 256), back.reshape(NG, 128, 256)


def per_device(density, images, block_tiles, image_blocks, shifts, precision):
    vol_at = lax.axis_index("vol")
    img_at = lax.axis_index("img")
    score_t, back_t = phase_tables()
    score_t = lax.dynamic_slice_in_dim(jnp.asarray(score_t), img_at, 1, 0)
    back_t = lax.dynamic_slice_in_dim(jnp.asarray(back_t), img_at, 1, 0)
    smem = pl.BlockSpec(memory_space=pltpu.SMEM)
    vmem = pl.BlockSpec(memory_space=pltpu.VMEM)

    idx = (image_blocks[:, :, None] * 32 + shifts[:, None, :] + 8).reshape(NG, 2 * TR)
    params = jnp.concatenate(
        [idx.astype(F32), precision[:, None], jnp.zeros((NG, 127 - 2 * TR), F32)], axis=1
    )
    params = params.reshape(4, 2, 128).transpose(1, 0, 2).reshape(8, 128)

    one = call(
        first_kernel,
        struct((NG, 104, 128)),
        "third_index",
        in_specs=[smem, vmem, vmem, vmem, vmem],
    )(
        vol_at.reshape(1).astype(jnp.int32),
        density,
        table_first(),
        block_tiles.reshape(NV, NB, ROWS),
        params,
    )
    images, one = lax.optimization_barrier((images, one))
    lists = over_img(one)

    shared = call(
        image_kernel,
        struct((NG, 4, ROWS, 128), BF),
        "image_split",
        grid=(4,),
        in_specs=[pl.BlockSpec((2, 2, ROWS, N), lambda i: (i, 0, 0, 0))],
        out_specs=pl.BlockSpec((NG, 1, ROWS, 128), lambda i: (0, i, 0, 0)),
    )(images)
    lists, shared = lax.optimization_barrier((lists, shared))
    two = call(second_kernel, struct((NV, 8, 128)), "second_index")(lists, table_second())
    two = over_vol(two)
    two, shared = lax.optimization_barrier((two, shared))
    shared = over_img(shared)

    fourier, outgoing = call(
        gather_kernel,
        (struct((2, N, 128)), struct((NV, 64, 128), BF)),
        "slice_tiles",
        scratch_shapes=[pltpu.VMEM((N, N), BF)],
    )(two, table_third(), jnp.asarray(table_fold(), BF), lists)
    incoming = over_vol(outgoing).reshape(NV, 4, CAP, 128)

    def whole_spec(shape):
        return pl.BlockSpec(shape, lambda i: (0,) * len(shape))

    image_spec = pl.BlockSpec((2, 4, ROWS, 128), lambda i: (i, 0, 0, 0))
    slot_spec = pl.BlockSpec((NV, 1, CAP, 128), lambda i: (0, i, 0, 0))
    partial = call(
        score_kernel,
        struct((NG, 16, 128)),
        "score",
        grid=(4,),
        in_specs=[
            image_spec,
            slot_spec,
            whole_spec((NG, 104, 128)),
            whole_spec((1, 2, 128, 256)),
        ],
        out_specs=whole_spec((NG, 16, 128)),
        scratch_shapes=[pltpu.VMEM((NB, 64, 128), F32)] * 3,
    )(shared, incoming, lists, score_t)
    partial = over_img(partial)

    weights, back = call(
        back_kernel,
        (struct((64, 128)), struct((NV, 72, 128), BF)),
        "backproject",
        grid=(4,),
        in_specs=[
            image_spec,
            whole_spec((NG, 16, 128)),
            whole_spec((NG, 104, 128)),
            whole_spec((1, 128, 256)),
        ],
        out_specs=(whole_spec((64, 128)), whole_spec((NV, 72, 128))),
        scratch_shapes=[
            pltpu.VMEM((NB, 64, 128), F32),
            pltpu.VMEM((NB, 64, 128), F32),
            pltpu.VMEM((512, 128), BF),
        ],
    )(shared, partial, lists, back_t)
    returned = over_vol(back)

    updated = call(
        total_kernel,
        struct((NG, 2, FJ, 128)),
        "totals",
        scratch_shapes=[
            pltpu.VMEM((N, N), F32),
            pltpu.VMEM((N, 8), F32),
            pltpu.VMEM((NV, 128), jnp.int32),
            pltpu.VMEM((NV, 128), F32),
        ],
    )(returned, fourier, jnp.asarray(table_spread(), BF), lists)
    updated = over_img(updated)
    updated = call(last_kernel, struct((SLAB, FJ, 2, N)), "frequency_join")(updated)

    own = lax.dynamic_slice_in_dim(weights, img_at * 8, 8, 0)[:, : 2 * TR]
    posterior = own.reshape(2, 4, 2, TR).transpose(1, 0, 2, 3).reshape(NG, 2, TR)
    return (updated, posterior)


def solution(mesh):
    in_specs = (
        P("vol", "img", None),
        P(("img", "vol"), None, None, None),
        P("img", None),
        P(("img", "vol"), None),
        P(("img", "vol"), None),
        P(("img", "vol")),
    )
    out_specs = (P("vol", "img", None, None), P(("img", "vol"), None, None))
    return jax.shard_map(
        per_device, mesh=mesh, in_specs=in_specs, out_specs=out_specs, check_vma=False
    )
```

```python
import functools
import math

import jax
import jax.numpy as jnp
import numpy as np
from jax import lax
from jax.experimental import pallas as pl
from jax.experimental.pallas import tpu as pltpu
from jax.sharding import PartitionSpec as P

N = 256
NG = 8
NV = 64
SLAB = 4
NB = 4
ROWS = 128
CAP = 16
FJ = N // NG
UNROLL = 2
TR = 16
F32 = jnp.float32
BF = jnp.bfloat16
HI = lax.Precision.HIGHEST
VM = 100 * 1024 * 1024 // 2


def dot32(a, b):
    return jnp.dot(a, b, precision=HI, preferred_element_type=F32)


def dot16(a, b):
    return jnp.dot(a, b, preferred_element_type=F32)


def dot_nt(a, b, precision=None):
    return lax.dot_general(
        a, b, (((1,), (1,)), ((), ())), precision=precision, preferred_element_type=F32
    )


def lanes(shape):
    return lax.broadcasted_iota(jnp.int32, shape, len(shape) - 1)


def swap4(parts):
    group = lanes(parts[0].shape) // 32
    out = []
    for b in range(4):
        acc = None
        for a in range(4):
            shift = (32 * (a - b)) % 128
            moved = parts[a] if shift == 0 else pltpu.roll(parts[a], shift, 1)
            acc = moved if acc is None else jnp.where(group == a, moved, acc)
        out.append(acc)
    return out


def table_first():
    n = np.arange(N)
    ang = 2.0 * np.pi * ((n[:, None] * n[None, :]) % N) / N
    return np.concatenate([np.cos(ang), -np.sin(ang)], axis=1).astype(np.float32)


def table_second():
    k = np.arange(N).reshape(NV, SLAB)
    n = np.arange(N)
    ang = 2.0 * np.pi * ((k[:, :, None] * n[None, None, :]) % N) / N
    c, s = np.cos(ang), np.sin(ang)
    left = np.stack([c, -s], axis=1).reshape(2 * N, N)
    right = np.stack([s, c], axis=1).reshape(2 * N, N)
    return np.stack([left, right]).astype(np.float32)


def table_third():
    k = np.arange(N)
    n = (np.arange(NV)[None, :] * 4 + np.arange(4)[:, None]).reshape(-1)
    ang = 2.0 * np.pi * ((k[:, None] * n[None, :]) % N) / N
    scale = float(N) ** -1.5
    return np.stack([np.cos(ang) * scale, np.sin(ang) * scale]).astype(np.float32)


def table_fold():
    out = np.zeros((2, 4, 32, 2, 2, 32), np.float32)
    for c in range(2):
        for j in range(32):
            out[c, :, j, :, c, j] = 1.0
    return out.reshape(256, 128)


def table_spread():
    out = np.zeros((2, 2, 2, 32, 2, 4, 32), np.float32)
    for h in range(2):
        for c in range(2):
            for j in range(32):
                out[h, h, c, j, c, :, j] = 1.0
    return out.reshape(2, 128, 256)


def fill_lists(at_ref, tiles_ref, blocks_ref, shifts_ref, prec_ref, o_ref):
    tiles = jnp.concatenate([tiles_ref[pl.ds(b, NV, stride=NB), :] for b in range(NB)], axis=1)
    at = at_ref[0]
    width = NB * ROWS
    lane = lanes((NV, width))
    sub = lax.broadcasted_iota(jnp.int32, (NV, width), 0)
    earlier = jnp.where(
        lax.broadcasted_iota(jnp.int32, (width, width), 0) < lanes((width, width)), 1.0, 0.0
    ).astype(BF)

    owned = jnp.right_shift(tiles, 10) == at
    rank = dot16(jnp.where(owned, 1.0, 0.0).astype(BF), earlier).astype(jnp.int32)
    coded = jnp.bitwise_and(tiles, 1023) + jnp.right_shift(lane, 7) * 1024 + 1
    rank = jnp.where(owned, rank, -1)
    short = lanes((NV, 128))
    table = jnp.zeros((NV, 128), F32)
    for s in range(CAP):
        code = jnp.sum(jnp.where(rank == s, coded, 0).astype(F32), axis=1, keepdims=True)
        table = jnp.where(short == s, code, table)
    table = jnp.concatenate([table, table], axis=0) - 1.0
    codes = table.T[:CAP]

    mine = jnp.concatenate(
        [tiles_ref[pl.ds(at * NB + b, 1), :] for b in range(NB)], axis=1
    )
    owner = jnp.right_shift(mine, 10)
    hot = sub == owner
    count = dot16(jnp.where(hot, 1.0, 0.0).astype(BF), earlier)
    place = jnp.sum(jnp.where(hot, count, 0.0), axis=0, keepdims=True).astype(jnp.int32)
    pos = owner * CAP + place
    row = lanes((8, width))
    kind = lax.broadcasted_iota(jnp.int32, (8, width), 0)
    digits = jnp.where(
        kind == 0, jnp.right_shift(row, 5), jnp.where(kind == 1, jnp.bitwise_and(row, 31), 1)
    ).astype(F32).astype(BF)
    found = jnp.where(
        lax.broadcasted_iota(jnp.int32, (NV * CAP, width), 0) == pos, 1.0, 0.0
    ).astype(BF)
    read = dot_nt(digits, found)
    inv = read[0:1] * 32.0 + read[1:2] + read[2:3] - 1.0
    pos = pos.astype(F32)
    moved = (shifts_ref[...] + 8).astype(F32)
    eye = (lanes((8, 8)) == lax.broadcasted_iota(jnp.int32, (8, 8), 0)).astype(F32)
    blocks = dot_nt(eye, blocks_ref[...].astype(F32), HI)
    params = jnp.concatenate(
        [
            blocks[:, 0:1] * 32.0 + moved,
            blocks[:, 1:2] * 32.0 + moved,
            dot_nt(eye, prec_ref[...], HI),
            jnp.zeros((8, 127 - 2 * TR), F32),
        ],
        axis=1,
    )
    for k in range(NG):
        o_ref[k, 64:80] = codes
        for q in range(8):
            o_ref[k, 80 + q : 81 + q] = inv[:, q * 128 : q * 128 + 128]
        for q in range(4):
            o_ref[k, 88 + q : 89 + q] = pos[:, q * 128 : q * 128 + 128]
        o_ref[k, 92:96] = jnp.zeros((4, 128), F32)
        o_ref[k, 96:104] = params


def first_kernel(
    at_ref, d_hbm, t_hbm, tiles_hbm, blocks_hbm, shifts_hbm, prec_hbm, o_ref,
    d_ref, t_ref, tiles_ref, blocks_ref, shifts_ref, prec_ref, sems,
):
    pairs = (
        (tiles_hbm, tiles_ref),
        (blocks_hbm, blocks_ref),
        (shifts_hbm, shifts_ref),
        (prec_hbm, prec_ref),
        (t_hbm, t_ref),
        (d_hbm, d_ref),
    )
    copies = [pltpu.make_async_copy(a, b, sems.at[k]) for k, (a, b) in enumerate(pairs)]
    for copy in copies:
        copy.start()
    for copy in copies[:4]:
        copy.wait()
    fill_lists(at_ref, tiles_ref, blocks_ref, shifts_ref, prec_ref, o_ref)
    for copy in copies[4:]:
        copy.wait()
    table = t_ref[...]
    rows = [dot32(d_ref[n0], table) for n0 in range(4)]
    for c in range(2):
        for hi in range(2):
            at = c * N + hi * 128
            moved = swap4([rows[n0][:, at : at + 128] for n0 in range(4)])
            for lo in range(4):
                o_ref[hi * 4 + lo, c * 32 : c * 32 + 32] = moved[lo]


def second_kernel(x_ref, w_ref, o_ref):
    re = x_ref[:, 0:32].reshape(N, 128)
    im = x_ref[:, 32:64].reshape(N, 128)
    o_ref[...] = (dot32(w_ref[0], re) + dot32(w_ref[1], im)).reshape(NV, 8, 128)


def slot_columns(lists_ref):
    low = lanes((CAP, 128)) < 64
    rows = [
        jnp.where(low, lists_ref[2 * gh, 64:80], lists_ref[2 * gh + 1, 64:80]) for gh in range(4)
    ]
    return jnp.concatenate(rows, axis=0).astype(jnp.int32)


def slot_rows(lists_ref):
    by_slot = jnp.concatenate(
        [lists_ref[2 * gh + h, 64:80] for h in range(2) for gh in range(4)], axis=0
    )
    return by_slot.T[:NV].astype(jnp.int32)


def gather_kernel(x_ref, w_ref, fold_ref, lists_ref, f_ref, o_hbm, half, o_ref, sems):
    parts = []
    for c in range(2):
        moved = swap4([x_ref[:, c * 4 + k, :] for k in range(4)])
        parts.append(jnp.concatenate(moved, axis=0))
    cos_t, sin_t = w_ref[0], w_ref[1]
    f_re = dot32(cos_t, parts[0]) + dot32(sin_t, parts[1])
    f_im = dot32(cos_t, parts[1]) - dot32(sin_t, parts[0])
    f_ref[0] = f_re
    f_ref[1] = f_im
    half[:, :128] = f_re.astype(BF)
    half[:, 128:] = f_im.astype(BF)

    columns = slot_columns(lists_ref)

    def step(nb, carry):
        cols = pltpu.roll(columns, 128 - 4 * nb, 1)
        tile = jnp.concatenate(
            [
                jnp.broadcast_to(cols[:, 64 * h + v : 64 * h + v + 1], (64, 128))
                for v in range(4)
                for h in range(2)
            ],
            axis=0,
        )
        lane = lanes(tile.shape)
        k0 = jnp.bitwise_and(tile, N - 1)
        k1 = jnp.where(tile < 0, -1, jnp.bitwise_and(jnp.right_shift(tile, 8), 3))
        hot = jnp.concatenate(
            [jnp.where(k0 == lane, 1.0, 0.0), jnp.where(k0 == lane + 128, 1.0, 0.0)], axis=1
        ).astype(BF)
        got = dot16(hot, half[...])
        keep = k1 == lane // 32
        kept = jnp.concatenate(
            [jnp.where(keep, got[:, :128], 0.0), jnp.where(keep, got[:, 128:], 0.0)], axis=1
        ).astype(BF)
        packed = dot16(kept, fold_ref[...]).reshape(4, 2, 64, 128)
        low = lanes((4, 64, 128)) < 64
        at = pl.ds(nb * 4, 4)
        o_ref[at] = jnp.where(low, packed[:, 0], packed[:, 1]).astype(BF)
        pltpu.make_async_copy(o_ref.at[at], o_hbm.at[at], sems.at[nb]).start()
        return carry

    lax.fori_loop(0, 16, step, 0, unroll=UNROLL)
    for nb in range(16):
        at = pl.ds(nb * 4, 4)
        pltpu.make_async_copy(o_ref.at[at], o_hbm.at[at], sems.at[nb]).wait()


def image_kernel(at_ref, x_ref, o_ref):
    at = at_ref[0]
    chip, core = at // 2, at % 2
    for hi in range(2):
        parts = [
            x_ref[a // 2, a % 2, :, hi * 128 : hi * 128 + 128].astype(F32) for a in range(4)
        ]
        moved = swap4(parts)
        for lo in range(4):
            target = hi * 4 + lo
            other = jnp.where(core == target % 2, 0, 1)
            o_ref[other, jnp.bitwise_and(target // 2 - chip, 3), 0] = moved[lo].astype(BF)


def score_kernel(at_ref, x0, x1, x2, x3, s_ref, lists_ref, t_ref, o_ref, cp1, cp2, ce):
    chip, core = at_ref[0] // 2, at_ref[0] % 2
    half_of = lanes((512, 128)) // 64
    for k in range(8):
        x_ref = (x0, x1, x2, x3)[k // 2]
        rel = k % 2
        gh = jnp.bitwise_and(chip - k // 2, 3)
        h = jnp.bitwise_xor(core, rel)
        g = gh * 2 + h
        at = pl.ds(pl.multiple_of(gh * CAP, CAP), CAP)
        data = s_ref[:, at, :].reshape(NV * CAP, 128)
        inv = lists_ref[g, 80:88].astype(jnp.int32)
        sub = lax.broadcasted_iota(jnp.int32, (512, 128), 0)
        hot = jnp.concatenate(
            [jnp.where(sub == inv[q : q + 1], 1.0, 0.0).astype(BF) for q in range(8)], axis=1
        )
        got = dot16(hot, data)
        got = jnp.where(half_of == h, got, 0.0)
        rows = got + pltpu.roll(got, 64, 1)
        turned = pltpu.roll(rows, 32, 1)
        for b in range(NB):
            s_a = rows[b * ROWS : (b + 1) * ROWS]
            s_b = turned[b * ROWS : (b + 1) * ROWS]
            energy = jnp.sum(s_a * s_a, axis=0, keepdims=True)
            for ih in range(4):
                image = x_ref[rel, ih].astype(F32)
                one = jnp.sum(s_a * image, axis=0, keepdims=True)
                two = jnp.sum(s_b * image, axis=0, keepdims=True)
                for lo in range(2):
                    at = pl.ds(g * 8 + ih * 2 + lo, 1)
                    cp1[b, at, :] = one
                    cp2[b, at, :] = two
                    ce[b, at, :] = energy

    full = (
        dot32(cp1[...].reshape(256, 128), t_ref[0, 0])
        + dot32(cp2[...].reshape(256, 128), t_ref[0, 1])
        + dot32(ce[...].reshape(256, 128), jnp.full((128, 256), -0.25, F32))
    ).reshape(NB, 64, 256)
    group = lanes((64, 128)) // 32
    first = lax.broadcasted_iota(jnp.int32, (64, 128), 0) % 2 == 0
    table = jnp.zeros((64, 128), F32)
    for b in range(NB):
        own = jnp.where(first, full[b, :, :128], full[b, :, 128:])
        table = jnp.where(group == b, own, table)
    idx = lists_ref[:, 96:104].reshape(64, 128).astype(jnp.int32)
    score = jnp.take_along_axis(table, jnp.bitwise_and(idx, 127), axis=1)
    group = lanes((16, 128)) // 32
    packed = score[:16]
    for q in range(1, 4):
        packed = jnp.where(group == q, pltpu.roll(score[q * 16 : q * 16 + 16], 32 * q, 1), packed)
    for k in range(NG):
        o_ref[k] = packed


def back_kernel(at_ref, x0, x1, x2, x3, p_ref, lists_ref, u_ref, w_ref, o_ref, fr, fi, rows):
    chip, core = at_ref[0] // 2, at_ref[0] % 2
    if True:
        packed = p_ref[0]
        for k in range(1, NG):
            packed = packed + p_ref[k]
        score = jnp.concatenate(
            [packed if q == 0 else pltpu.roll(packed, 128 - 32 * q, 1) for q in range(4)], axis=0
        )
        lane = lanes((64, 128))
        valid = lane < 2 * TR
        params = lists_ref[:, 96:104].reshape(64, 128)
        logits = score * params[:, 32:33]
        top = jnp.max(jnp.where(valid, logits, -jnp.inf), axis=1, keepdims=True)
        expo = jnp.where(valid, jnp.exp(jnp.where(valid, logits - top, 0.0)), 0.0)
        post = expo / jnp.sum(expo, axis=1, keepdims=True)
        w_ref[...] = post
        idx = params.astype(jnp.int32)
        weight = jnp.zeros((64, 128), F32)
        for k in range(2 * TR):
            weight = weight + jnp.where(lane == idx[:, k : k + 1], post[:, k : k + 1], 0.0)
        group = lane // 32
        stacked = jnp.concatenate(
            [jnp.where(group == b, weight, 0.0) for b in range(NB)], axis=0
        )
        fac = dot32(stacked, u_ref[0]).reshape(NB, 64, 256)
        low = lane < 64
        for b in range(NB):
            for part, ref in ((0, fr), (1, fi)):
                val = fac[b, :, part * 128 : part * 128 + 128]
                val = jnp.where(low, val, pltpu.roll(val, 63, 0))
                ref[b] = val.astype(BF).astype(F32)
        block_of = (
            lanes((8, 128)) // 32 == lax.broadcasted_iota(jnp.int32, (8, 128), 0)
        ).astype(F32)
        per_image = dot_nt(block_of, weight, HI)
        sub = lax.broadcasted_iota(jnp.int32, (64, 128), 0)
        per_group = dot32(per_image, (sub // 8 == lane % 32 // 4).astype(F32))
        sub = lax.broadcasted_iota(jnp.int32, (8, 128), 0)
        lane = lanes((8, 128))
        mass = jnp.sum(jnp.where(sub == lane % 4, per_group, 0.0), axis=0, keepdims=True)
        upper = mass.astype(BF).astype(F32)
        middle = (mass - upper).astype(BF).astype(F32)
        piece = lanes((1, 128)) // 32
        mass = jnp.where(
            piece == 0,
            upper,
            jnp.where(piece == 1, middle, jnp.where(piece == 2, mass - upper - middle, 0.0)),
        )
        o_ref[:, 64:72] = jnp.broadcast_to(mass.reshape(1, 1, 128), (NV, 8, 128)).astype(BF)

    half_of = lanes((NV * CAP, 128)) // 64
    for d in range(4):
        x_ref = (x0, x1, x2, x3)[d]
        gh = jnp.bitwise_and(chip - d, 3)
        outs = []
        for rel in range(2):
            g = gh * 2 + jnp.bitwise_xor(core, rel)
            for b in range(NB):
                acc_a = jnp.zeros((ROWS, 128), F32)
                acc_b = jnp.zeros((ROWS, 128), F32)
                for ih in range(4):
                    image = x_ref[rel, ih].astype(F32)
                    at = pl.ds(g * 8 + ih * 2, 1)
                    acc_a = acc_a + image * fr[b, at, :]
                    acc_b = acc_b + image * fi[b, at, :]
                acc = acc_a + pltpu.roll(acc_a, 64, 1)
                acc_b = acc_b + pltpu.roll(acc_b, 64, 1)
                rows[rel, b * ROWS : (b + 1) * ROWS] = (acc + pltpu.roll(acc_b, 32, 1)).astype(BF)
            pos = lists_ref[g, 88:92].astype(jnp.int32)
            sub = lax.broadcasted_iota(jnp.int32, (NV * CAP, 128), 0)
            hot = jnp.concatenate(
                [jnp.where(sub == pos[q : q + 1], 1.0, 0.0).astype(BF) for q in range(4)], axis=1
            )
            outs.append(dot16(hot, rows[rel]))
        at = pl.ds(pl.multiple_of(gh * CAP, CAP), CAP)
        out = jnp.where(half_of == core, outs[0], outs[1])
        o_ref[:, at, :] = out.astype(BF).reshape(NV, CAP, 128)


def total_kernel(x_ref, f_ref, spread_ref, lists_ref, o_ref, tot, codes):
    tot[...] = jnp.zeros_like(tot)
    columns = slot_columns(lists_ref)
    codes[...] = slot_rows(lists_ref)

    def step(nb, carry):
        cols = pltpu.roll(columns, 128 - 4 * nb, 1)
        data = x_ref[pl.ds(nb * 4, 4), 0:64, :].reshape(256, 128)
        kept = []
        for h in range(2):
            col = jnp.concatenate(
                [
                    jnp.broadcast_to(cols[:, 64 * h + v : 64 * h + v + 1], (64, 128))
                    for v in range(4)
                ],
                axis=0,
            )
            k1 = jnp.where(col < 0, -1, jnp.bitwise_and(jnp.right_shift(col, 8), 3))
            keep = k1 == lanes((256, 128)) // 32
            wide = dot16(data, spread_ref[h])
            kept.append(
                jnp.concatenate(
                    [jnp.where(keep, wide[:, :128], 0.0), jnp.where(keep, wide[:, 128:], 0.0)],
                    axis=1,
                ).astype(BF)
            )
        kept = jnp.concatenate(
            [kept[h][v * 64 : v * 64 + 64] for v in range(4) for h in range(2)], axis=0
        )
        sub = lax.broadcasted_iota(jnp.int32, (N, 128), 0)
        hot = jnp.concatenate(
            [
                jnp.where(
                    sub == jnp.bitwise_and(codes[pl.ds(nb * 4 + v, 1), :], N - 1), 1.0, 0.0
                ).astype(BF)
                for v in range(4)
            ],
            axis=1,
        )
        tot[...] += dot16(hot, kept)
        return carry

    lax.fori_loop(0, 16, step, 0, unroll=UNROLL)
    for c in range(2):
        new = (tot[:, c * 128 : c * 128 + 128] + f_ref[c]).astype(BF)
        o_ref[:, c] = new.reshape(NG, FJ, 128)


def mass_kernel(at_ref, sent_ref, lists_ref, o_ref):
    code = slot_rows(lists_ref)
    sent = sent_ref[:, 0, :].astype(F32)
    source = lax.broadcasted_iota(jnp.int32, (128, 128), 0)
    target = lanes((128, 128))
    group = target % 64 // 16 * 2 + target // 64
    mass = jnp.zeros((NV, 128), F32)
    for b in range(NB):
        pick = (source % 32 == group * 4 + b).astype(F32)
        mass = jnp.where(jnp.right_shift(code, 10) == b, dot32(sent, pick), mass)
    sub = lax.broadcasted_iota(jnp.int32, (FJ, 128), 0) + at_ref[0] * FJ
    total = [jnp.zeros((FJ, 128), F32) for _ in range(SLAB)]
    for v in range(NV):
        row = code[v : v + 1]
        k1 = jnp.where(row < 0, -1, jnp.bitwise_and(jnp.right_shift(row, 8), 3))
        hot = sub == jnp.bitwise_and(row, N - 1)
        for k in range(SLAB):
            share = jnp.where(k1 == k, mass[v : v + 1], 0.0)
            total[k] = total[k] + jnp.where(hot, share, 0.0)
    lane = lanes((FJ, 128))
    out = jnp.ones((FJ, 128), F32)
    for k in range(SLAB):
        out = jnp.where(lane == k, 1.0 + jnp.sum(total[k], axis=1, keepdims=True), out)
    o_ref[...] = out


def last_kernel(x_ref, m_ref, o_ref):
    scale = 1.0 / m_ref[...]
    for c in range(2):
        for hi in range(2):
            moved = swap4([x_ref[hi * 4 + lo, c].astype(F32) for lo in range(4)])
            for k in range(4):
                o_ref[k, :, c, hi * 128 : hi * 128 + 128] = moved[k] * scale[:, k : k + 1]


def call(kernel, out, name, vmem_bytes=VM, **extra):
    return pl.pallas_call(
        kernel,
        out_shape=out,
        name=name,
        compiler_params=pltpu.CompilerParams(vmem_limit_bytes=vmem_bytes),
        **extra,
    )


def struct(shape, dtype=F32):
    return jax.ShapeDtypeStruct(shape, dtype)


def over_img(x):
    return lax.all_to_all(x, "img", split_axis=0, concat_axis=0, tiled=True)


def over_vol(x):
    return lax.all_to_all(x, "vol", split_axis=0, concat_axis=0, tiled=True)


def phase_tables():
    freq = np.arange(N).reshape(NG, FJ)
    shift = np.arange(32) - 8
    ang = 2.0 * np.pi * ((freq[:, :, None] * shift[None, None, :]) % N) / N
    cos_t, sin_t = np.cos(ang), np.sin(ang)
    score = np.zeros((NG, 2, 2, 2, FJ, 2, NB, 32), np.float32)
    back = np.zeros((NG, NB, 32, 2, 2, 2, FJ), np.float32)
    for c in range(2):
        sign = 1.0 if c else -1.0
        for lo in range(2):
            score[:, 0, lo, c, :, lo] = cos_t[:, :, None, :]
            score[:, 1, lo, c, :, lo] = sign * sin_t[:, :, None, :]
            back[:, :, :, 0, lo, c, :] = cos_t.transpose(0, 2, 1)[:, None]
            back[:, :, :, 1, lo, c, :] = sign * sin_t.transpose(0, 2, 1)[:, None]
    return score.reshape(NG, 2, 128, 256), back.reshape(NG, 128, 256)


def per_device(density, images, block_tiles, image_blocks, shifts, precision):
    vol_at = lax.axis_index("vol")
    img_at = lax.axis_index("img")
    score_t, back_t = phase_tables()
    score_t = lax.dynamic_slice_in_dim(jnp.asarray(score_t), img_at, 1, 0)
    back_t = lax.dynamic_slice_in_dim(jnp.asarray(back_t), img_at, 1, 0)
    smem = pl.BlockSpec(memory_space=pltpu.SMEM)
    vmem = pl.BlockSpec(memory_space=pltpu.VMEM)
    hbm = pl.BlockSpec(memory_space=pltpu.HBM)

    one = call(
        first_kernel,
        struct((NG, 104, 128)),
        "third_index",
        vmem_bytes=63 * 1000 * 1000,
        in_specs=[smem] + [hbm] * 6,
        scratch_shapes=[
            pltpu.VMEM((4, FJ, N), F32),
            pltpu.VMEM((N, 2 * N), F32),
            pltpu.VMEM((NV * NB, ROWS), jnp.int32),
            pltpu.VMEM((2, NG), jnp.int32),
            pltpu.VMEM((NG, TR), jnp.int32),
            pltpu.VMEM((1, NG), F32),
            pltpu.SemaphoreType.DMA((6,)),
        ],
    )(
        vol_at.reshape(1).astype(jnp.int32),
        density,
        table_first(),
        block_tiles,
        image_blocks.T,
        shifts,
        precision.reshape(1, NG),
    )
    images, one = lax.optimization_barrier((images, one))
    lists = over_img(one)

    own_at = img_at.reshape(1).astype(jnp.int32)
    shared = call(
        image_kernel,
        struct((2, 4, 4, ROWS, 128), BF),
        "image_split",
        grid=(4,),
        in_specs=[smem, pl.BlockSpec((2, 2, ROWS, N), lambda i: (i, 0, 0, 0))],
        out_specs=pl.BlockSpec((2, 4, 1, ROWS, 128), lambda i: (0, 0, i, 0, 0)),
    )(own_at, images)
    lists, shared = lax.optimization_barrier((lists, shared))
    sibling = lax.ppermute(shared[1], "img", [(i, i ^ 1) for i in range(NG)])
    pairs = jnp.stack([shared[0], sibling], axis=1)
    two = call(second_kernel, struct((NV, 8, 128)), "second_index")(lists, table_second())
    two = over_vol(two)
    two, pairs = lax.optimization_barrier((two, pairs))

    fourier, outgoing = call(
        gather_kernel,
        (struct((2, N, 128)), struct((NV, 64, 128), BF)),
        "slice_tiles",
        in_specs=[vmem] * 4,
        out_specs=(vmem, hbm),
        scratch_shapes=[
            pltpu.VMEM((N, N), BF),
            pltpu.VMEM((NV, 64, 128), BF),
            pltpu.SemaphoreType.DMA((16,)),
        ],
    )(two, table_third(), jnp.asarray(table_fold(), BF), lists)
    outgoing, pairs = lax.optimization_barrier((outgoing, pairs))
    incoming = over_vol(outgoing)
    from_chip = [pairs[0]] + [
        lax.ppermute(pairs[d], "img", [(i, (i + 2 * d) % NG) for i in range(NG)])
        for d in range(1, 4)
    ]

    partial = call(
        score_kernel,
        struct((NG, 16, 128)),
        "score",
        in_specs=[smem] + [vmem] * 7,
        scratch_shapes=[pltpu.VMEM((NB, 64, 128), F32)] * 3,
    )(own_at, *from_chip, incoming, lists, score_t)
    partial = over_img(partial)

    weights, back = call(
        back_kernel,
        (struct((64, 128)), struct((NV, 72, 128), BF)),
        "backproject",
        in_specs=[smem] + [vmem] * 7,
        scratch_shapes=[
            pltpu.VMEM((NB, 64, 128), F32),
            pltpu.VMEM((NB, 64, 128), F32),
            pltpu.VMEM((2, 512, 128), BF),
        ],
    )(own_at, *from_chip, partial, lists, back_t)
    returned = over_vol(back)

    updated = call(
        total_kernel,
        struct((NG, 2, FJ, 128), BF),
        "totals",
        scratch_shapes=[pltpu.VMEM((N, N), F32), pltpu.VMEM((NV, 128), jnp.int32)],
    )(returned, fourier, jnp.asarray(table_spread(), BF), lists)
    sent = lax.slice_in_dim(returned, 64, 72, axis=1)
    sent, updated = lax.optimization_barrier((sent, updated))
    updated = over_img(updated)
    masses = call(
        mass_kernel, struct((FJ, 128)), "masses", in_specs=[smem, vmem, vmem]
    )(own_at, sent, lists)
    updated = call(last_kernel, struct((SLAB, FJ, 2, N)), "frequency_join")(updated, masses)

    own = lax.dynamic_slice_in_dim(weights, img_at * 8, 8, 0)[:, : 2 * TR]
    posterior = own.reshape(NG, 2, TR)
    return (updated, posterior)


def solution(mesh):
    in_specs = (
        P("vol", "img", None),
        P(("img", "vol"), None, None, None),
        P("img", None),
        P(("img", "vol"), None),
        P(("img", "vol"), None),
        P(("img", "vol")),
    )
    out_specs = (P("vol", "img", None, None), P(("img", "vol"), None, None))
    return jax.shard_map(
        per_device, mesh=mesh, in_specs=in_specs, out_specs=out_specs, check_vma=False
    )
```

```python
import functools
import math

import jax
import jax.numpy as jnp
import numpy as np
from jax import lax
from jax.experimental import pallas as pl
from jax.experimental.pallas import tpu as pltpu
from jax.sharding import PartitionSpec as P

N = 256
NG = 8
NV = 64
SLAB = 4
NB = 4
ROWS = 128
CAP = 16
FJ = N // NG
POOL = 48
UNROLL = 4
TR = 16
F32 = jnp.float32
BF = jnp.bfloat16
HI = lax.Precision.HIGHEST
VM = 24 * 1024 * 1024


def dot32(a, b):
    return jnp.dot(a, b, precision=HI, preferred_element_type=F32)


def dot16(a, b):
    return jnp.dot(a, b, preferred_element_type=F32)


def dot_nt(a, b, precision=None):
    return lax.dot_general(
        a, b, (((1,), (1,)), ((), ())), precision=precision, preferred_element_type=F32
    )


def one_hot(a, b):
    return jnp.where(a.astype(jnp.int16) == b.astype(jnp.int16), BF(1), BF(0))


def lanes(shape):
    return lax.broadcasted_iota(jnp.int32, shape, len(shape) - 1)


def swap4(parts):
    group = lanes(parts[0].shape) // 32
    out = []
    for b in range(4):
        acc = None
        for a in range(4):
            shift = (32 * (a - b)) % 128
            moved = parts[a] if shift == 0 else pltpu.roll(parts[a], shift, 1)
            acc = moved if acc is None else jnp.where(group == a, moved, acc)
        out.append(acc)
    return out


def table_first():
    n = np.arange(N)
    ang = 2.0 * np.pi * ((n[:, None] * n[None, :]) % N) / N
    return np.concatenate([np.cos(ang), -np.sin(ang)], axis=1).astype(np.float32)


def table_second():
    k = np.arange(N).reshape(NV, SLAB)
    n = np.arange(N)
    ang = 2.0 * np.pi * ((k[:, :, None] * n[None, None, :]) % N) / N
    c, s = np.cos(ang), np.sin(ang)
    left = np.stack([c, -s], axis=1).reshape(2 * N, N)
    right = np.stack([s, c], axis=1).reshape(2 * N, N)
    return np.stack([left, right]).astype(np.float32)


def table_third():
    k = np.arange(N)
    n = (np.arange(NV)[None, :] * 4 + np.arange(4)[:, None]).reshape(-1)
    ang = 2.0 * np.pi * ((k[:, None] * n[None, :]) % N) / N
    scale = float(N) ** -1.5
    return np.stack([np.cos(ang) * scale, np.sin(ang) * scale]).astype(np.float32)


def table_fold():
    out = np.zeros((2, 4, 32, 2, 2, 32), np.float32)
    for c in range(2):
        for j in range(32):
            out[c, :, j, :, c, j] = 1.0
    return out.reshape(256, 128)


def table_spread():
    out = np.zeros((2, 2, 2, 32, 2, 4, 32), np.float32)
    for h in range(2):
        for c in range(2):
            for j in range(32):
                out[h, h, c, j, c, :, j] = 1.0
    return out.reshape(2, 128, 256)


def quad_rows(table):
    group = lanes((16, 128)) // 32
    packed = table[:16]
    for q in range(1, 4):
        packed = jnp.where(group == q, pltpu.roll(table[q * 16 : q * 16 + 16], 32 * q, 1), packed)
    return packed


def fill_lists(at_ref, tiles_ref, blocks_ref, shifts_ref, prec_ref, o_ref):
    tiles = jnp.concatenate([tiles_ref[pl.ds(b, NV, stride=NB), :] for b in range(NB)], axis=1)
    at = at_ref[0]
    width = NB * ROWS
    lane = lanes((NV, width))
    sub = lax.broadcasted_iota(jnp.int32, (NV, width), 0)
    earlier = jnp.where(
        lax.broadcasted_iota(jnp.int32, (width, width), 0) < lanes((width, width)), 1.0, 0.0
    ).astype(BF)

    owned = jnp.right_shift(tiles, 10) == at
    rank = dot16(jnp.where(owned, 1.0, 0.0).astype(BF), earlier).astype(jnp.int32)
    coded = jnp.bitwise_and(tiles, 1023) + jnp.right_shift(lane, 7) * 1024 + 1
    rank = jnp.where(owned, rank, -1)
    short = lanes((NV, 128))
    table = jnp.zeros((NV, 128), F32)
    for s in range(CAP):
        code = jnp.sum(jnp.where(rank == s, coded, 0).astype(F32), axis=1, keepdims=True)
        table = jnp.where(short == s, code, table)
    table = jnp.concatenate([table, table], axis=0) - 1.0
    codes = table.T[:CAP]

    mine = jnp.concatenate(
        [tiles_ref[pl.ds(at * NB + b, 1), :] for b in range(NB)], axis=1
    )
    owner = jnp.right_shift(mine, 10)
    hot = sub == owner
    count = dot16(jnp.where(hot, 1.0, 0.0).astype(BF), earlier)
    place = jnp.sum(jnp.where(hot, count, 0.0), axis=0, keepdims=True).astype(jnp.int32)
    pos = owner * CAP + place
    row = lanes((8, width))
    kind = lax.broadcasted_iota(jnp.int32, (8, width), 0)
    digits = jnp.where(
        kind == 0, jnp.right_shift(row, 5), jnp.where(kind == 1, jnp.bitwise_and(row, 31), 1)
    ).astype(F32).astype(BF)
    found = jnp.where(
        lax.broadcasted_iota(jnp.int32, (NV * CAP, width), 0) == pos, 1.0, 0.0
    ).astype(BF)
    read = dot_nt(digits, found)
    inv = read[0:1] * 32.0 + read[1:2] + read[2:3] - 1.0
    pos = pos.astype(F32)
    wide = lax.broadcasted_iota(jnp.int32, (128, width), 0) == owner
    own_count = dot_nt(jnp.ones((8, width), BF), jnp.where(wide, 1.0, 0.0).astype(BF))
    owners = jnp.right_shift(tiles, 10)
    counts = jnp.zeros((NV, 128), F32)
    for k in range(NV):
        hits = jnp.where(owners == k, 1.0 if k < 32 else 256.0, 0.0)
        hits = hits[:, :128] + hits[:, 128:256] + hits[:, 256:384] + hits[:, 384:]
        hits = jnp.sum(hits, axis=1, keepdims=True)
        counts = jnp.where(short == k % 32, counts + hits, counts)
    pair_count = quad_rows(counts)
    moved = (shifts_ref[...] + 8).astype(F32)
    eye = (lanes((8, 8)) == lax.broadcasted_iota(jnp.int32, (8, 8), 0)).astype(F32)
    blocks = dot_nt(eye, blocks_ref[...].astype(F32), HI)
    params = jnp.concatenate(
        [
            blocks[:, 0:1] * 32.0 + moved,
            blocks[:, 1:2] * 32.0 + moved,
            dot_nt(eye, prec_ref[...], HI),
            jnp.zeros((8, 127 - 2 * TR), F32),
        ],
        axis=1,
    )
    for k in range(NG):
        o_ref[k, 64:80] = codes
        for q in range(8):
            o_ref[k, 80 + q : 81 + q] = inv[:, q * 128 : q * 128 + 128]
        for q in range(4):
            o_ref[k, 88 + q : 89 + q] = pos[:, q * 128 : q * 128 + 128]
        o_ref[k, 92:96] = own_count[0:4]
        o_ref[k, 96:104] = params
        o_ref[k, 104:120] = pair_count


def first_kernel(
    at_ref, d_hbm, t_hbm, tiles_hbm, blocks_hbm, shifts_hbm, prec_hbm, o_ref,
    d_ref, t_ref, tiles_ref, blocks_ref, shifts_ref, prec_ref, sems,
):
    pairs = (
        (tiles_hbm, tiles_ref),
        (blocks_hbm, blocks_ref),
        (shifts_hbm, shifts_ref),
        (prec_hbm, prec_ref),
        (t_hbm, t_ref),
        (d_hbm, d_ref),
    )
    copies = [pltpu.make_async_copy(a, b, sems.at[k]) for k, (a, b) in enumerate(pairs)]
    for copy in copies:
        copy.start()
    for copy in copies[:4]:
        copy.wait()
    fill_lists(at_ref, tiles_ref, blocks_ref, shifts_ref, prec_ref, o_ref)
    for copy in copies[4:]:
        copy.wait()
    table = t_ref[...]
    rows = [dot32(d_ref[n0], table) for n0 in range(4)]
    for c in range(2):
        for hi in range(2):
            at = c * N + hi * 128
            moved = swap4([rows[n0][:, at : at + 128] for n0 in range(4)])
            for lo in range(4):
                o_ref[hi * 4 + lo, c * 32 : c * 32 + 32] = moved[lo]


def second_kernel(x_ref, w_ref, o_ref):
    re = x_ref[:, 0:32].reshape(N, 128)
    im = x_ref[:, 32:64].reshape(N, 128)
    o_ref[...] = (dot32(w_ref[0], re) + dot32(w_ref[1], im)).reshape(NV, 8, 128)


def pool_kernel(lists_ref, cols_ref, offs_ref, flag_ref):
    before = (
        lanes((NG, NG)) < lax.broadcasted_iota(jnp.int32, (NG, NG), 0)
    ).astype(F32)
    counts = jnp.concatenate([lists_ref[g, 92:93] for g in range(NG)], axis=0)
    offs_ref[0] = jnp.minimum(dot32(before, counts).astype(jnp.int32), 2 * POOL)
    offs_ref[1] = lax.broadcasted_iota(jnp.int32, (NG, 128), 0) * CAP
    pairs = lists_ref[0, 104:120]
    for g in range(1, NG):
        pairs = pairs + lists_ref[g, 104:120]
    pairs = pairs.astype(jnp.int32)
    most = jnp.maximum(jnp.bitwise_and(pairs, 255), jnp.right_shift(pairs, 8))
    most = jnp.max(jnp.max(most, axis=0, keepdims=True), axis=1, keepdims=True)
    flag_ref[...] = jnp.broadcast_to(jnp.where(most <= 2 * POOL - 1, 1, 0), (8, 128))
    half = lanes((64, 128)) // 64
    row = lax.broadcasted_iota(jnp.int32, (64, 128), 0)
    place_a = jnp.where(row < POOL, row + half * POOL, -1)
    place_b = row + half * 64
    col_a = jnp.zeros((64, 128), jnp.int32)
    col_b = jnp.zeros((64, 128), jnp.int32)
    start = jnp.zeros((1, 128), jnp.int32)
    for g in range(NG):
        code = lists_ref[g, 64:80].astype(jnp.int32)
        filled = jnp.where(code >= 0, code + 1 + 4096 * g, 0)
        for s in range(CAP):
            col_a = col_a + jnp.where(place_a == start + s, filled[s : s + 1], 0)
            col_b = jnp.where(place_b == g * CAP + s, filled[s : s + 1], col_b)
        start = start + jnp.sum(jnp.where(code >= 0, 1, 0), axis=0, keepdims=True)
    cols_ref[0] = col_a - 1
    cols_ref[1] = col_b - 1


def slot_rows(columns):
    wide = jnp.concatenate([columns, columns], axis=0).astype(F32).T
    low = lanes((NV, 128)) < 64
    return jnp.where(low, wide[:NV], wide[NV:]).astype(jnp.int32)


def gather_kernel(x_ref, w_ref, fold_ref, cols_ref, f_ref, o_hbm, half, o_ref, sems):
    rows = o_ref.shape[1]
    parts = []
    for c in range(2):
        moved = swap4([x_ref[:, c * 4 + k, :] for k in range(4)])
        parts.append(jnp.concatenate(moved, axis=0))
    cos_t, sin_t = w_ref[0], w_ref[1]
    f_re = dot32(cos_t, parts[0]) + dot32(sin_t, parts[1])
    f_im = dot32(cos_t, parts[1]) - dot32(sin_t, parts[0])
    f_ref[0] = f_re
    f_ref[1] = f_im
    half[:, :128] = f_re.astype(BF)
    half[:, 128:] = f_im.astype(BF)

    columns = cols_ref[...]

    def step(nb, carry):
        cols = pltpu.roll(columns, 128 - 4 * nb, 1)
        tile = jnp.concatenate(
            [
                jnp.broadcast_to(cols[:rows, 64 * h + v : 64 * h + v + 1], (rows, 128))
                for v in range(4)
                for h in range(2)
            ],
            axis=0,
        )
        lane = lanes(tile.shape)
        k0 = jnp.bitwise_and(tile, N - 1)
        k1 = jnp.where(tile < 0, -1, jnp.bitwise_and(jnp.right_shift(tile, 8), 3))
        hot = jnp.concatenate(
            [one_hot(k0, lane), one_hot(k0, lane + 128)], axis=1
        )
        got = dot16(hot, half[...])
        keep = k1 == lane // 32
        kept = jnp.concatenate(
            [jnp.where(keep, got[:, :128], 0.0), jnp.where(keep, got[:, 128:], 0.0)], axis=1
        ).astype(BF)
        packed = dot16(kept, fold_ref[...]).reshape(4, 2, rows, 128)
        low = lanes((4, rows, 128)) < 64
        at = pl.ds(nb * 4, 4)
        o_ref[at] = jnp.where(low, packed[:, 0], packed[:, 1]).astype(BF)
        pltpu.make_async_copy(o_ref.at[at], o_hbm.at[at], sems.at[nb]).start()
        return carry

    lax.fori_loop(0, 16, step, 0, unroll=UNROLL)
    for nb in range(16):
        at = pl.ds(nb * 4, 4)
        pltpu.make_async_copy(o_ref.at[at], o_hbm.at[at], sems.at[nb]).wait()


def image_kernel(at_ref, x_ref, own_ref, other_ref):
    chip, core = at_ref[0] // 2, at_ref[0] % 2
    for hi in range(2):
        parts = [
            x_ref[a // 2, a % 2, :, hi * 128 : hi * 128 + 128].astype(F32) for a in range(4)
        ]
        moved = [part.astype(BF) for part in swap4(parts)]
        for lo in range(0, 4, 2):
            offset = jnp.bitwise_and(hi * 2 + lo // 2 - chip, 3)
            own_ref[offset, 0] = jnp.where(core == 0, moved[lo], moved[lo + 1])
            other_ref[offset, 0] = jnp.where(core == 0, moved[lo + 1], moved[lo])


def score_kernel(
    at_ref, offs_ref, x0, x1, x2, x3, s_ref, lists_ref, t_ref, o_ref, cp1, cp2, ce, pool, slots
):
    chip, core = at_ref[0] // 2, at_ref[0] % 2
    rows_in = s_ref.shape[1]
    low = lanes((8, rows_in, 128)) < 64

    def spread(n, carry):
        at = pl.ds(n * 8, 8)
        got = s_ref[at].astype(F32)
        back = pltpu.roll(got, 64, 2)
        pool[at, 0:rows_in] = jnp.where(low, got, back)
        pool[at, rows_in : 2 * rows_in] = jnp.where(low, back, got)
        pool[at, 2 * rows_in :] = jnp.zeros((8, CAP, 128), F32)
        return carry

    lax.fori_loop(0, 8, spread, 0)

    for k in range(8):
        x_ref = (x0, x1, x2, x3)[k // 2]
        rel = k % 2
        gh = jnp.bitwise_and(chip - k // 2, 3)
        h = jnp.bitwise_xor(core, rel)
        g = gh * 2 + h
        for v in range(NV):
            slots[v * CAP : (v + 1) * CAP] = pool[v, pl.ds(offs_ref[g, v], CAP), :].astype(BF)
        data = slots[...]
        inv = lists_ref[g, 80:88].astype(jnp.int32)
        sub = lax.broadcasted_iota(jnp.int32, (512, 128), 0)
        hot = jnp.concatenate(
            [one_hot(sub, inv[q : q + 1]) for q in range(8)], axis=1
        )
        rows = dot16(hot, data)
        turned = pltpu.roll(rows, 32, 1)
        parts = [slice(b * ROWS, (b + 1) * ROWS) for b in range(NB)]
        energy = [jnp.sum(rows[p] * rows[p], axis=0, keepdims=True) for p in parts]
        for ih in range(4):
            image = x_ref[rel, ih].astype(F32)
            for b in range(NB):
                one = jnp.sum(rows[parts[b]] * image, axis=0, keepdims=True)
                two = jnp.sum(turned[parts[b]] * image, axis=0, keepdims=True)
                for lo in range(2):
                    at = pl.ds(g * 8 + ih * 2 + lo, 1)
                    cp1[b, at, :] = one
                    cp2[b, at, :] = two
                    ce[b, at, :] = energy[b]

    full = (
        dot32(cp1[...].reshape(256, 128), t_ref[0, 0])
        + dot32(cp2[...].reshape(256, 128), t_ref[0, 1])
        + dot32(ce[...].reshape(256, 128), jnp.full((128, 256), -0.25, F32))
    ).reshape(NB, 64, 256)
    group = lanes((64, 128)) // 32
    first = lax.broadcasted_iota(jnp.int32, (64, 128), 0) % 2 == 0
    table = jnp.zeros((64, 128), F32)
    for b in range(NB):
        own = jnp.where(first, full[b, :, :128], full[b, :, 128:])
        table = jnp.where(group == b, own, table)
    idx = lists_ref[:, 96:104].reshape(64, 128).astype(jnp.int32)
    score = jnp.take_along_axis(table, jnp.bitwise_and(idx, 127), axis=1)
    packed = quad_rows(score)
    for k in range(NG):
        o_ref[k] = packed


def back_kernel(
    at_ref, offs_ref, x0, x1, x2, x3, p_ref, lists_ref, u_ref, w_ref, o_ref, fr, fi, rows, pool
):
    chip, core = at_ref[0] // 2, at_ref[0] % 2
    if True:
        packed = p_ref[0]
        for k in range(1, NG):
            packed = packed + p_ref[k]
        score = jnp.concatenate(
            [packed if q == 0 else pltpu.roll(packed, 128 - 32 * q, 1) for q in range(4)], axis=0
        )
        lane = lanes((64, 128))
        valid = lane < 2 * TR
        params = lists_ref[:, 96:104].reshape(64, 128)
        logits = score * params[:, 32:33]
        top = jnp.max(jnp.where(valid, logits, -jnp.inf), axis=1, keepdims=True)
        expo = jnp.where(valid, jnp.exp(jnp.where(valid, logits - top, 0.0)), 0.0)
        post = expo / jnp.sum(expo, axis=1, keepdims=True)
        w_ref[...] = post
        idx = params.astype(jnp.int32)
        weight = jnp.zeros((64, 128), F32)
        for k in range(2 * TR):
            weight = weight + jnp.where(lane == idx[:, k : k + 1], post[:, k : k + 1], 0.0)
        group = lane // 32
        stacked = jnp.concatenate(
            [jnp.where(group == b, weight, 0.0) for b in range(NB)], axis=0
        )
        fac = dot32(stacked, u_ref[0]).reshape(NB, 64, 256)
        low = lane < 64
        for b in range(NB):
            for part, ref in ((0, fr), (1, fi)):
                val = fac[b, :, part * 128 : part * 128 + 128]
                val = jnp.where(low, val, pltpu.roll(val, 63, 0))
                ref[b] = val.astype(BF).astype(F32)
        block_of = (
            lanes((8, 128)) // 32 == lax.broadcasted_iota(jnp.int32, (8, 128), 0)
        ).astype(F32)
        per_image = dot_nt(block_of, weight, HI)
        sub = lax.broadcasted_iota(jnp.int32, (64, 128), 0)
        per_group = dot32(per_image, (sub // 8 == lane % 32 // 4).astype(F32))
        sub = lax.broadcasted_iota(jnp.int32, (8, 128), 0)
        lane = lanes((8, 128))
        mass = jnp.sum(jnp.where(sub == lane % 4, per_group, 0.0), axis=0, keepdims=True)
        upper = mass.astype(BF).astype(F32)
        mass = jnp.where(lanes((1, 128)) // 32 == 2, upper, mass - upper)

    pool[...] = jnp.zeros_like(pool)
    for d in range(4):
        x_ref = (x0, x1, x2, x3)[d]
        gh = jnp.bitwise_and(chip - d, 3)
        for rel in range(2):
            g = gh * 2 + jnp.bitwise_xor(core, rel)
            for part in range(0, ROWS, 32):
                images = [x_ref[rel, ih, part : part + 32].astype(F32) for ih in range(4)]
                for b in range(NB):
                    acc_a = jnp.zeros((32, 128), F32)
                    acc_b = jnp.zeros((32, 128), F32)
                    for ih in range(4):
                        at = pl.ds(g * 8 + ih * 2, 1)
                        acc_a = acc_a + images[ih] * fr[b, at, :]
                        acc_b = acc_b + images[ih] * fi[b, at, :]
                    acc = acc_a + pltpu.roll(acc_a, 64, 1)
                    acc_b = acc_b + pltpu.roll(acc_b, 64, 1)
                    first = b * ROWS + part
                    rows[rel, first : first + 32] = (acc + pltpu.roll(acc_b, 32, 1)).astype(BF)
            pos = lists_ref[g, 88:92].astype(jnp.int32)
            sub = lax.broadcasted_iota(jnp.int32, (NV * CAP, 128), 0)
            hot = jnp.concatenate(
                [one_hot(sub, pos[q : q + 1]) for q in range(4)], axis=1
            )
            out = dot16(hot, rows[rel])
            for v in range(NV):
                at = pl.ds(offs_ref[g, v], CAP)
                pool[v, at, :] = pool[v, at, :] + out[v * CAP : (v + 1) * CAP]
    half_rows = (pool.shape[1] - CAP) // 2
    low = lanes((8, half_rows, 128)) < 64
    last = lax.broadcasted_iota(jnp.int32, (8, half_rows, 128), 1) == half_rows - 1
    tight = half_rows == POOL

    def fold(n, carry):
        at = pl.ds(n * 8, 8)
        out = jnp.where(low, pool[at, 0:half_rows], pool[at, half_rows : 2 * half_rows])
        if tight:
            out = jnp.where(last & jnp.logical_not(low), mass.reshape(1, 1, 128), out)
        o_ref[at, 0:half_rows] = out.astype(BF)
        return carry

    lax.fori_loop(0, 8, fold, 0)
    if not tight:
        o_ref[:, half_rows:] = jnp.broadcast_to(mass.reshape(1, 1, 128), (NV, 8, 128)).astype(BF)


def total_kernel(x_ref, f_ref, spread_ref, cols_ref, o_ref, tot, codes):
    tot[...] = jnp.zeros_like(tot)
    columns = cols_ref[...]
    codes[...] = slot_rows(columns)
    tight = x_ref.shape[1] == POOL

    def step(nb, carry):
        cols = pltpu.roll(columns, 128 - 4 * nb, 1)
        if tight:
            fill = jnp.zeros((4, 64 - POOL, 128), BF)
            data = jnp.concatenate([x_ref[pl.ds(nb * 4, 4)], fill], axis=1).reshape(256, 128)
        else:
            data = x_ref[pl.ds(nb * 4, 4), 0:64, :].reshape(256, 128)
        kept = []
        for h in range(2):
            col = jnp.concatenate(
                [
                    jnp.broadcast_to(cols[:, 64 * h + v : 64 * h + v + 1], (64, 128))
                    for v in range(4)
                ],
                axis=0,
            )
            k1 = jnp.where(col < 0, -1, jnp.bitwise_and(jnp.right_shift(col, 8), 3))
            keep = k1 == lanes((256, 128)) // 32
            wide = dot16(data, spread_ref[h])
            kept.append(
                jnp.concatenate(
                    [jnp.where(keep, wide[:, :128], 0.0), jnp.where(keep, wide[:, 128:], 0.0)],
                    axis=1,
                ).astype(BF)
            )
        kept = jnp.concatenate(
            [kept[h][v * 64 : v * 64 + 64] for v in range(4) for h in range(2)], axis=0
        )
        sub = lax.broadcasted_iota(jnp.int32, (N, 128), 0)
        hot = jnp.concatenate(
            [
                one_hot(sub, jnp.bitwise_and(codes[pl.ds(nb * 4 + v, 1), :], N - 1))
                for v in range(4)
            ],
            axis=1,
        )
        tot[...] += dot16(hot, kept)
        return carry

    lax.fori_loop(0, 16, step, 0, unroll=UNROLL)
    for c in range(2):
        new = (tot[:, c * 128 : c * 128 + 128] + f_ref[c]).astype(BF)
        o_ref[:, c] = new.reshape(NG, FJ, 128)


def mass_kernel(at_ref, sent_ref, cols_ref, o_ref):
    code = slot_rows(cols_ref[...])
    sent = sent_ref[:, 0, :].astype(F32)
    block = jnp.right_shift(code, 10)
    sent = sent + pltpu.roll(sent, 96, 1)
    mass = jnp.take_along_axis(sent, jnp.where(code >= 0, 64 + block, 0), axis=1)
    sub = lax.broadcasted_iota(jnp.int32, (FJ, 128), 0) + at_ref[0] * FJ
    total = [jnp.zeros((FJ, 128), F32) for _ in range(SLAB)]
    for v in range(NV):
        row = code[v : v + 1]
        k1 = jnp.where(row < 0, -1, jnp.bitwise_and(jnp.right_shift(row, 8), 3))
        hot = sub == jnp.bitwise_and(row, N - 1)
        for k in range(SLAB):
            share = jnp.where(k1 == k, mass[v : v + 1], 0.0)
            total[k] = total[k] + jnp.where(hot, share, 0.0)
    lane = lanes((FJ, 128))
    out = jnp.ones((FJ, 128), F32)
    for k in range(SLAB):
        out = jnp.where(lane == k, 1.0 + jnp.sum(total[k], axis=1, keepdims=True), out)
    o_ref[...] = out


def last_kernel(x_ref, m_ref, o_ref):
    scale = 1.0 / m_ref[...]
    for c in range(2):
        for hi in range(2):
            moved = swap4([x_ref[hi * 4 + lo, c].astype(F32) for lo in range(4)])
            for k in range(4):
                o_ref[k, :, c, hi * 128 : hi * 128 + 128] = moved[k] * scale[:, k : k + 1]


def call(kernel, out, name, vmem_bytes=VM, **extra):
    return pl.pallas_call(
        kernel,
        out_shape=out,
        name=name,
        compiler_params=pltpu.CompilerParams(vmem_limit_bytes=vmem_bytes),
        **extra,
    )


def struct(shape, dtype=F32):
    return jax.ShapeDtypeStruct(shape, dtype)


def over_img(x):
    return lax.all_to_all(x, "img", split_axis=0, concat_axis=0, tiled=True)


def over_vol(x):
    return lax.all_to_all(x, "vol", split_axis=0, concat_axis=0, tiled=True)


def phase_tables():
    freq = np.arange(N).reshape(NG, FJ)
    shift = np.arange(32) - 8
    ang = 2.0 * np.pi * ((freq[:, :, None] * shift[None, None, :]) % N) / N
    cos_t, sin_t = np.cos(ang), np.sin(ang)
    score = np.zeros((NG, 2, 2, 2, FJ, 2, NB, 32), np.float32)
    back = np.zeros((NG, NB, 32, 2, 2, 2, FJ), np.float32)
    for c in range(2):
        sign = 1.0 if c else -1.0
        for lo in range(2):
            score[:, 0, lo, c, :, lo] = cos_t[:, :, None, :]
            score[:, 1, lo, c, :, lo] = sign * sin_t[:, :, None, :]
            back[:, :, :, 0, lo, c, :] = cos_t.transpose(0, 2, 1)[:, None]
            back[:, :, :, 1, lo, c, :] = sign * sin_t.transpose(0, 2, 1)[:, None]
    return score.reshape(NG, 2, 128, 256), back.reshape(NG, 128, 256)


def pipeline(half_rows, density, images, block_tiles, image_blocks, shifts, precision):
    vol_at = lax.axis_index("vol")
    img_at = lax.axis_index("img")
    score_t, back_t = phase_tables()
    score_t = lax.dynamic_slice_in_dim(jnp.asarray(score_t), img_at, 1, 0)
    back_t = lax.dynamic_slice_in_dim(jnp.asarray(back_t), img_at, 1, 0)
    smem = pl.BlockSpec(memory_space=pltpu.SMEM)
    vmem = pl.BlockSpec(memory_space=pltpu.VMEM)
    hbm = pl.BlockSpec(memory_space=pltpu.HBM)

    one = call(
        first_kernel,
        struct((NG, 120, 128)),
        "third_index",
        vmem_bytes=63 * 1000 * 1000,
        in_specs=[smem] + [hbm] * 6,
        scratch_shapes=[
            pltpu.VMEM((4, FJ, N), F32),
            pltpu.VMEM((N, 2 * N), F32),
            pltpu.VMEM((NV * NB, ROWS), jnp.int32),
            pltpu.VMEM((2, NG), jnp.int32),
            pltpu.VMEM((NG, TR), jnp.int32),
            pltpu.VMEM((1, NG), F32),
            pltpu.SemaphoreType.DMA((6,)),
        ],
    )(
        vol_at.reshape(1).astype(jnp.int32),
        density,
        table_first(),
        block_tiles,
        image_blocks.T,
        shifts,
        precision.reshape(1, NG),
    )
    images, one = lax.optimization_barrier((images, one))
    lists = over_img(one)

    own_at = img_at.reshape(1).astype(jnp.int32)
    own, other = call(
        image_kernel,
        (struct((4, 4, ROWS, 128), BF),) * 2,
        "image_split",
        grid=(4,),
        in_specs=[smem, pl.BlockSpec((2, 2, ROWS, N), lambda i: (i, 0, 0, 0))],
        out_specs=(pl.BlockSpec((4, 1, ROWS, 128), lambda i: (0, i, 0, 0)),) * 2,
    )(own_at, images)
    lists, own, other = lax.optimization_barrier((lists, own, other))
    two = call(second_kernel, struct((NV, 8, 128)), "second_index")(lists, table_second())
    two, lists, other = lax.optimization_barrier((two, lists, other))
    cols, offs, flag = call(
        pool_kernel,
        (
            struct((2, 64, 128), jnp.int32),
            struct((2, NG, 128), jnp.int32),
            struct((8, 128), jnp.int32),
        ),
        "pools",
    )(lists)
    cols, other = lax.optimization_barrier((cols, other))
    sibling = lax.ppermute(other, "img", [(i, i ^ 1) for i in range(NG)])
    pairs = jnp.stack([own, sibling], axis=1)
    two = over_vol(two)
    two, pairs = lax.optimization_barrier((two, pairs))

    return exchange(half_rows, own_at, two, pairs, lists, cols, offs, score_t, back_t), flag


def per_device(*inputs):
    img_at = lax.axis_index("img")
    done, flag = pipeline(POOL, *inputs)
    updated, weights = lax.cond(
        flag[0, 0] > 0,
        lambda done, *rest: done,
        lambda done, *rest: pipeline(64, *rest)[0],
        done,
        *inputs,
    )
    own = lax.dynamic_slice_in_dim(weights, img_at * 8, 8, 0)[:, : 2 * TR]
    posterior = own.reshape(NG, 2, TR)
    return (updated, posterior)


def exchange(rows, own_at, two, pairs, lists, cols, offs, score_t, back_t):
    smem = pl.BlockSpec(memory_space=pltpu.SMEM)
    vmem = pl.BlockSpec(memory_space=pltpu.VMEM)
    hbm = pl.BlockSpec(memory_space=pltpu.HBM)
    tight = rows == POOL
    cols = cols[0 if tight else 1]
    offs = offs[0 if tight else 1]
    fourier, outgoing = call(
        gather_kernel,
        (struct((2, N, 128)), struct((NV, rows, 128), BF)),
        "slice_tiles",
        in_specs=[vmem] * 4,
        out_specs=(vmem, hbm),
        scratch_shapes=[
            pltpu.VMEM((N, N), BF),
            pltpu.VMEM((NV, rows, 128), BF),
            pltpu.SemaphoreType.DMA((16,)),
        ],
    )(two, table_third(), jnp.asarray(table_fold(), BF), cols)
    outgoing, pairs = lax.optimization_barrier((outgoing, pairs))
    incoming = over_vol(outgoing)
    from_chip = [pairs[0]] + [
        lax.ppermute(pairs[d], "img", [(i, (i + 2 * d) % NG) for i in range(NG)])
        for d in range(1, 4)
    ]
    partial = call(
        score_kernel,
        struct((NG, 16, 128)),
        "score",
        in_specs=[smem] * 2 + [vmem] * 7,
        scratch_shapes=[pltpu.VMEM((NB, 64, 128), F32)] * 3
        + [pltpu.VMEM((NV, 2 * rows + CAP, 128), F32), pltpu.VMEM((NV * CAP, 128), BF)],
    )(own_at, offs, *from_chip, incoming, lists, score_t)
    partial = over_img(partial)

    weights, back = call(
        back_kernel,
        (struct((64, 128)), struct((NV, rows if tight else rows + 8, 128), BF)),
        "backproject",
        in_specs=[smem] * 2 + [vmem] * 7,
        scratch_shapes=[
            pltpu.VMEM((NB, 64, 128), F32),
            pltpu.VMEM((NB, 64, 128), F32),
            pltpu.VMEM((2, 512, 128), BF),
            pltpu.VMEM((NV, 2 * rows + CAP, 128), F32),
        ],
    )(own_at, offs, *from_chip, partial, lists, back_t)
    returned = over_vol(back)

    updated = call(
        total_kernel,
        struct((NG, 2, FJ, 128), BF),
        "totals",
        scratch_shapes=[pltpu.VMEM((N, N), F32), pltpu.VMEM((NV, 128), jnp.int32)],
    )(returned, fourier, jnp.asarray(table_spread(), BF), cols)
    at = rows - 1 if tight else rows
    sent = jnp.broadcast_to(lax.slice_in_dim(returned, at, at + 1, axis=1), (NV, 8, 128))
    sent, updated = lax.optimization_barrier((sent, updated))
    updated = over_img(updated)
    masses = call(
        mass_kernel, struct((FJ, 128)), "masses", in_specs=[smem, vmem, vmem]
    )(own_at, sent, cols)
    updated = call(last_kernel, struct((SLAB, FJ, 2, N)), "frequency_join")(updated, masses)
    return updated, weights


def solution(mesh):
    in_specs = (
        P("vol", "img", None),
        P(("img", "vol"), None, None, None),
        P("img", None),
        P(("img", "vol"), None),
        P(("img", "vol"), None),
        P(("img", "vol")),
    )
    out_specs = (P("vol", "img", None, None), P(("img", "vol"), None, None))
    return jax.shard_map(
        per_device, mesh=mesh, in_specs=in_specs, out_specs=out_specs, check_vma=False
    )
```

```python
import functools
import math

import jax
import jax.numpy as jnp
import numpy as np
from jax import lax
from jax.experimental import pallas as pl
from jax.experimental.pallas import tpu as pltpu
from jax.sharding import PartitionSpec as P

N = 256
NG = 8
NV = 64
SLAB = 4
NB = 4
ROWS = 128
CAP = 16
FJ = N // NG
POOL = 48
UNROLL = 4
TR = 16
F32 = jnp.float32
BF = jnp.bfloat16
HI = lax.Precision.HIGHEST
VM = 24 * 1024 * 1024


def dot32(a, b):
    return jnp.dot(a, b, precision=HI, preferred_element_type=F32)


def dot16(a, b):
    return jnp.dot(a, b, preferred_element_type=F32)


def dot_nt(a, b, precision=None):
    return lax.dot_general(
        a, b, (((1,), (1,)), ((), ())), precision=precision, preferred_element_type=F32
    )


def one_hot(a, b):
    return jnp.where(a.astype(jnp.int16) == b.astype(jnp.int16), BF(1), BF(0))


def lanes(shape):
    return lax.broadcasted_iota(jnp.int32, shape, len(shape) - 1)


def swap4(parts):
    group = lanes(parts[0].shape) // 32
    out = []
    for b in range(4):
        acc = None
        for a in range(4):
            shift = (32 * (a - b)) % 128
            moved = parts[a] if shift == 0 else pltpu.roll(parts[a], shift, 1)
            acc = moved if acc is None else jnp.where(group == a, moved, acc)
        out.append(acc)
    return out


def table_first():
    n = np.arange(N)
    ang = 2.0 * np.pi * ((n[:, None] * n[None, :]) % N) / N
    return np.concatenate([np.cos(ang), -np.sin(ang)], axis=1).astype(np.float32)


def table_second():
    k = np.arange(N).reshape(NV, SLAB)
    n = np.arange(N)
    ang = 2.0 * np.pi * ((k[:, :, None] * n[None, None, :]) % N) / N
    c, s = np.cos(ang), np.sin(ang)
    left = np.stack([c, -s], axis=1).reshape(2 * N, N)
    right = np.stack([s, c], axis=1).reshape(2 * N, N)
    return np.stack([left, right]).astype(np.float32)


def table_third():
    k = np.arange(N)
    n = (np.arange(NV)[None, :] * 4 + np.arange(4)[:, None]).reshape(-1)
    ang = 2.0 * np.pi * ((k[:, None] * n[None, :]) % N) / N
    scale = float(N) ** -1.5
    return np.stack([np.cos(ang) * scale, np.sin(ang) * scale]).astype(np.float32)


def table_fold():
    out = np.zeros((2, 4, 32, 2, 2, 32), np.float32)
    for c in range(2):
        for j in range(32):
            out[c, :, j, :, c, j] = 1.0
    return out.reshape(256, 128)


def table_spread():
    out = np.zeros((2, 2, 2, 32, 2, 4, 32), np.float32)
    for h in range(2):
        for c in range(2):
            for j in range(32):
                out[h, h, c, j, c, :, j] = 1.0
    return out.reshape(2, 128, 256)


def quad_rows(table):
    group = lanes((16, 128)) // 32
    packed = table[:16]
    for q in range(1, 4):
        packed = jnp.where(group == q, pltpu.roll(table[q * 16 : q * 16 + 16], 32 * q, 1), packed)
    return packed


def fill_lists(at_ref, tiles_ref, blocks_ref, shifts_ref, prec_ref, o_ref):
    tiles = jnp.concatenate([tiles_ref[pl.ds(b, NV, stride=NB), :] for b in range(NB)], axis=1)
    at = at_ref[0]
    width = NB * ROWS
    lane = lanes((NV, width))
    sub = lax.broadcasted_iota(jnp.int32, (NV, width), 0)
    earlier = jnp.where(
        lax.broadcasted_iota(jnp.int32, (width, width), 0).astype(jnp.int16)
        < lanes((width, width)).astype(jnp.int16),
        BF(1),
        BF(0),
    )

    owned = jnp.right_shift(tiles, 10) == at
    rank = dot16(jnp.where(owned, 1.0, 0.0).astype(BF), earlier).astype(jnp.int32)
    coded = jnp.bitwise_and(tiles, 1023) + jnp.right_shift(lane, 7) * 1024 + 1
    rank = jnp.where(owned, rank, -1)
    short = lanes((NV, 128))
    table = jnp.zeros((NV, 128), F32)
    for s in range(CAP):
        code = jnp.sum(jnp.where(rank == s, coded, 0).astype(F32), axis=1, keepdims=True)
        table = jnp.where(short == s, code, table)
    table = jnp.concatenate([table, table], axis=0) - 1.0
    codes = table.T[:CAP]

    mine = jnp.concatenate(
        [tiles_ref[pl.ds(at * NB + b, 1), :] for b in range(NB)], axis=1
    )
    owner = jnp.right_shift(mine, 10)
    hot = sub == owner
    count = dot16(jnp.where(hot, 1.0, 0.0).astype(BF), earlier)
    place = jnp.sum(jnp.where(hot, count, 0.0), axis=0, keepdims=True).astype(jnp.int32)
    pos = owner * CAP + place
    row = lanes((8, width))
    kind = lax.broadcasted_iota(jnp.int32, (8, width), 0)
    digits = jnp.where(
        kind == 0, jnp.right_shift(row, 5), jnp.where(kind == 1, jnp.bitwise_and(row, 31), 1)
    ).astype(F32).astype(BF)
    found = one_hot(lax.broadcasted_iota(jnp.int32, (NV * CAP, width), 0), pos)
    read = dot_nt(digits, found)
    inv = read[0:1] * 32.0 + read[1:2] + read[2:3] - 1.0
    pos = pos.astype(F32)
    wide = lax.broadcasted_iota(jnp.int32, (128, width), 0) == owner
    own_count = dot_nt(jnp.ones((8, width), BF), jnp.where(wide, 1.0, 0.0).astype(BF))
    owners = jnp.right_shift(tiles, 10)
    counts = jnp.zeros((NV, 128), F32)
    for k in range(32):
        hits = jnp.where(owners == k, 1.0, jnp.where(owners == k + 32, 256.0, 0.0))
        hits = hits[:, :128] + hits[:, 128:256] + hits[:, 256:384] + hits[:, 384:]
        hits = jnp.sum(hits, axis=1, keepdims=True)
        counts = jnp.where(short == k, hits, counts)
    pair_count = quad_rows(counts)
    moved = (shifts_ref[...] + 8).astype(F32)
    eye = (lanes((8, 8)) == lax.broadcasted_iota(jnp.int32, (8, 8), 0)).astype(F32)
    blocks = dot_nt(eye, blocks_ref[...].astype(F32), HI)
    params = jnp.concatenate(
        [
            blocks[:, 0:1] * 32.0 + moved,
            blocks[:, 1:2] * 32.0 + moved,
            dot_nt(eye, prec_ref[...], HI),
            jnp.zeros((8, 127 - 2 * TR), F32),
        ],
        axis=1,
    )
    for k in range(NG):
        o_ref[k, 64:80] = codes
        for q in range(8):
            o_ref[k, 80 + q : 81 + q] = inv[:, q * 128 : q * 128 + 128]
        for q in range(4):
            o_ref[k, 88 + q : 89 + q] = pos[:, q * 128 : q * 128 + 128]
        o_ref[k, 92:96] = own_count[0:4]
        o_ref[k, 96:104] = params
        o_ref[k, 104:120] = pair_count


def first_kernel(
    at_ref, d_hbm, t_hbm, tiles_hbm, blocks_hbm, shifts_hbm, prec_hbm, o_ref,
    d_ref, t_ref, tiles_ref, blocks_ref, shifts_ref, prec_ref, sems,
):
    pairs = (
        (tiles_hbm, tiles_ref),
        (blocks_hbm, blocks_ref),
        (shifts_hbm, shifts_ref),
        (prec_hbm, prec_ref),
        (t_hbm, t_ref),
        (d_hbm, d_ref),
    )
    copies = [pltpu.make_async_copy(a, b, sems.at[k]) for k, (a, b) in enumerate(pairs)]
    for copy in copies:
        copy.start()
    for copy in copies[:4]:
        copy.wait()
    fill_lists(at_ref, tiles_ref, blocks_ref, shifts_ref, prec_ref, o_ref)
    for copy in copies[4:]:
        copy.wait()
    table = t_ref[...]
    rows = [dot32(d_ref[n0], table) for n0 in range(4)]
    for c in range(2):
        for hi in range(2):
            at = c * N + hi * 128
            moved = swap4([rows[n0][:, at : at + 128] for n0 in range(4)])
            for lo in range(4):
                o_ref[hi * 4 + lo, c * 32 : c * 32 + 32] = moved[lo]


def second_kernel(x_ref, w_ref, o_ref):
    re = x_ref[:, 0:32].reshape(N, 128)
    im = x_ref[:, 32:64].reshape(N, 128)
    o_ref[...] = (dot32(w_ref[0], re) + dot32(w_ref[1], im)).reshape(NV, 8, 128)


def pool_kernel(lists_ref, table_ref, cols_ref, offs_ref, flag_ref, near_ref):
    near_ref[...] = table_ref[...]
    before = (
        lanes((NG, NG)) < lax.broadcasted_iota(jnp.int32, (NG, NG), 0)
    ).astype(F32)
    counts = jnp.concatenate([lists_ref[g, 92:93] for g in range(NG)], axis=0)
    offs_ref[0] = jnp.minimum(dot32(before, counts).astype(jnp.int32), 2 * POOL)
    offs_ref[1] = lax.broadcasted_iota(jnp.int32, (NG, 128), 0) * CAP
    pairs = lists_ref[0, 104:120]
    for g in range(1, NG):
        pairs = pairs + lists_ref[g, 104:120]
    pairs = pairs.astype(jnp.int32)
    most = jnp.maximum(jnp.bitwise_and(pairs, 255), jnp.right_shift(pairs, 8))
    most = jnp.max(jnp.max(most, axis=0, keepdims=True), axis=1, keepdims=True)
    flag_ref[...] = jnp.broadcast_to(jnp.where(most <= 2 * POOL - 1, 1, 0), (8, 128))
    half = lanes((64, 128)) // 64
    row = lax.broadcasted_iota(jnp.int32, (64, 128), 0)
    place_a = jnp.where(row < POOL, row + half * POOL, -1)
    place_b = row + half * 64
    col_a = jnp.zeros((64, 128), jnp.int32)
    col_b = jnp.zeros((64, 128), jnp.int32)
    start = jnp.zeros((1, 128), jnp.int32)
    for g in range(NG):
        code = lists_ref[g, 64:80].astype(jnp.int32)
        filled = jnp.where(code >= 0, code + 1 + 4096 * g, 0)
        for s in range(CAP):
            col_a = col_a + jnp.where(place_a == start + s, filled[s : s + 1], 0)
            col_b = jnp.where(place_b == g * CAP + s, filled[s : s + 1], col_b)
        start = start + jnp.sum(jnp.where(code >= 0, 1, 0), axis=0, keepdims=True)
    cols_ref[0] = col_a - 1
    cols_ref[1] = col_b - 1


def slot_rows(columns):
    wide = jnp.concatenate([columns, columns], axis=0).astype(F32).T
    low = lanes((NV, 128)) < 64
    return jnp.where(low, wide[:NV], wide[NV:]).astype(jnp.int32)


def gather_kernel(x_ref, w_ref, fold_ref, cols_ref, f_ref, o_hbm, half, o_ref, sems):
    rows = o_ref.shape[1]
    parts = []
    for c in range(2):
        moved = swap4([x_ref[:, c * 4 + k, :] for k in range(4)])
        parts.append(jnp.concatenate(moved, axis=0))
    cos_t, sin_t = w_ref[0], w_ref[1]
    f_re = dot32(cos_t, parts[0]) + dot32(sin_t, parts[1])
    f_im = dot32(cos_t, parts[1]) - dot32(sin_t, parts[0])
    f_ref[0] = f_re
    f_ref[1] = f_im
    half[:, :128] = f_re.astype(BF)
    half[:, 128:] = f_im.astype(BF)

    columns = cols_ref[...]
    columns = jnp.where(columns < 0, -1, jnp.bitwise_and(columns, 1023))

    def step(nb, carry):
        cols = pltpu.roll(columns, 128 - 4 * nb, 1)
        tile = jnp.concatenate(
            [
                jnp.broadcast_to(cols[:rows, 64 * h + v : 64 * h + v + 1], (rows, 128))
                for v in range(4)
                for h in range(2)
            ],
            axis=0,
        )
        lane = lanes(tile.shape)
        k0 = jnp.bitwise_and(tile, N - 1)
        k1 = jnp.right_shift(tile, 8)
        hot = jnp.concatenate(
            [one_hot(k0, lane), one_hot(k0, lane + 128)], axis=1
        )
        got = dot16(hot, half[...])
        keep = k1 == lane // 32
        kept = jnp.concatenate(
            [jnp.where(keep, got[:, :128], 0.0), jnp.where(keep, got[:, 128:], 0.0)], axis=1
        ).astype(BF)
        packed = dot16(kept, fold_ref[...]).reshape(4, 2, rows, 128)
        low = lanes((4, rows, 128)) < 64
        at = pl.ds(nb * 4, 4)
        o_ref[at] = jnp.where(low, packed[:, 0], packed[:, 1]).astype(BF)
        pltpu.make_async_copy(o_ref.at[at], o_hbm.at[at], sems.at[nb]).start()
        return carry

    lax.fori_loop(0, 16, step, 0, unroll=UNROLL)
    for nb in range(16):
        at = pl.ds(nb * 4, 4)
        pltpu.make_async_copy(o_ref.at[at], o_hbm.at[at], sems.at[nb]).wait()


def image_kernel(at_ref, x_ref, own_ref, other_ref):
    chip, core = at_ref[0] // 2, at_ref[0] % 2
    for hi in range(2):
        parts = [
            x_ref[a // 2, a % 2, :, hi * 128 : hi * 128 + 128].astype(F32) for a in range(4)
        ]
        moved = [part.astype(BF) for part in swap4(parts)]
        for lo in range(0, 4, 2):
            offset = jnp.bitwise_and(hi * 2 + lo // 2 - chip, 3)
            own_ref[offset, 0] = jnp.where(core == 0, moved[lo], moved[lo + 1])
            other_ref[offset, 0] = jnp.where(core == 0, moved[lo + 1], moved[lo])


def score_kernel(
    at_ref, offs_ref, x0, x1, x2, x3, s_ref, lists_ref, t_ref, o_ref, cp1, cp2, ce, pool, slots
):
    chip, core = at_ref[0] // 2, at_ref[0] % 2
    rows_in = s_ref.shape[1]
    low = lanes((8, rows_in, 128)) < 64

    def spread(n, carry):
        at = pl.ds(n * 8, 8)
        got = s_ref[at].astype(F32)
        back = pltpu.roll(got, 64, 2)
        pool[at, 0:rows_in] = jnp.where(low, got, back)
        pool[at, rows_in : 2 * rows_in] = jnp.where(low, back, got)
        pool[at, 2 * rows_in :] = jnp.zeros((8, CAP, 128), F32)
        return carry

    lax.fori_loop(0, 8, spread, 0)

    for k in range(8):
        x_ref = (x0, x1, x2, x3)[k // 2]
        rel = k % 2
        gh = jnp.bitwise_and(chip - k // 2, 3)
        h = jnp.bitwise_xor(core, rel)
        g = gh * 2 + h
        for v in range(NV):
            slots[v * CAP : (v + 1) * CAP] = pool[v, pl.ds(offs_ref[g, v], CAP), :].astype(BF)
        data = slots[...]
        inv = lists_ref[g, 80:88].astype(jnp.int32)
        sub = lax.broadcasted_iota(jnp.int32, (512, 128), 0)
        hot = jnp.concatenate(
            [one_hot(sub, inv[q : q + 1]) for q in range(8)], axis=1
        )
        rows = dot16(hot, data)
        turned = pltpu.roll(rows, 32, 1)
        parts = [slice(b * ROWS, (b + 1) * ROWS) for b in range(NB)]
        energy = [jnp.sum(rows[p] * rows[p], axis=0, keepdims=True) for p in parts]
        for ih in range(4):
            image = x_ref[rel, ih].astype(F32)
            for b in range(NB):
                one = jnp.sum(rows[parts[b]] * image, axis=0, keepdims=True)
                two = jnp.sum(turned[parts[b]] * image, axis=0, keepdims=True)
                for lo in range(2):
                    at = pl.ds(g * 8 + ih * 2 + lo, 1)
                    cp1[b, at, :] = one
                    cp2[b, at, :] = two
                    ce[b, at, :] = energy[b]

    full = (
        dot32(cp1[...].reshape(256, 128), t_ref[0, 0])
        + dot32(cp2[...].reshape(256, 128), t_ref[0, 1])
        + dot32(ce[...].reshape(256, 128), jnp.full((128, 256), -0.25, F32))
    ).reshape(NB, 64, 256)
    group = lanes((64, 128)) // 32
    first = lax.broadcasted_iota(jnp.int32, (64, 128), 0) % 2 == 0
    table = jnp.zeros((64, 128), F32)
    for b in range(NB):
        own = jnp.where(first, full[b, :, :128], full[b, :, 128:])
        table = jnp.where(group == b, own, table)
    idx = lists_ref[:, 96:104].reshape(64, 128).astype(jnp.int32)
    score = jnp.take_along_axis(table, jnp.bitwise_and(idx, 127), axis=1)
    packed = quad_rows(score)
    for k in range(NG):
        o_ref[k] = packed


def back_kernel(
    at_ref, offs_ref, x0, x1, x2, x3, p_ref, lists_ref, u_ref, w_ref, o_ref, fr, fi, rows, pool
):
    chip, core = at_ref[0] // 2, at_ref[0] % 2
    if True:
        packed = p_ref[0]
        for k in range(1, NG):
            packed = packed + p_ref[k]
        score = jnp.concatenate(
            [packed if q == 0 else pltpu.roll(packed, 128 - 32 * q, 1) for q in range(4)], axis=0
        )
        lane = lanes((64, 128))
        valid = lane < 2 * TR
        params = lists_ref[:, 96:104].reshape(64, 128)
        logits = score * params[:, 32:33]
        top = jnp.max(jnp.where(valid, logits, -jnp.inf), axis=1, keepdims=True)
        expo = jnp.where(valid, jnp.exp(jnp.where(valid, logits - top, 0.0)), 0.0)
        post = expo / jnp.sum(expo, axis=1, keepdims=True)
        w_ref[...] = post
        idx = params.astype(jnp.int32)
        weight = jnp.zeros((64, 128), F32)
        for k in range(2 * TR):
            weight = weight + jnp.where(lane == idx[:, k : k + 1], post[:, k : k + 1], 0.0)
        group = lane // 32
        stacked = jnp.concatenate(
            [jnp.where(group == b, weight, 0.0) for b in range(NB)], axis=0
        )
        fac = dot32(stacked, u_ref[0]).reshape(NB, 64, 256)
        low = lane < 64
        for b in range(NB):
            for part, ref in ((0, fr), (1, fi)):
                val = fac[b, :, part * 128 : part * 128 + 128]
                val = jnp.where(low, val, pltpu.roll(val, 63, 0))
                ref[b] = val.astype(BF).astype(F32)
        block_of = (
            lanes((8, 128)) // 32 == lax.broadcasted_iota(jnp.int32, (8, 128), 0)
        ).astype(F32)
        per_image = dot_nt(block_of, weight, HI)
        sub = lax.broadcasted_iota(jnp.int32, (64, 128), 0)
        per_group = dot32(per_image, (sub // 8 == lane % 32 // 4).astype(F32))
        sub = lax.broadcasted_iota(jnp.int32, (8, 128), 0)
        lane = lanes((8, 128))
        mass = jnp.sum(jnp.where(sub == lane % 4, per_group, 0.0), axis=0, keepdims=True)
        upper = mass.astype(BF).astype(F32)
        mass = jnp.where(lanes((1, 128)) // 32 == 2, upper, mass - upper)

    pool[...] = jnp.zeros_like(pool)
    for d in range(4):
        x_ref = (x0, x1, x2, x3)[d]
        gh = jnp.bitwise_and(chip - d, 3)
        for rel in range(2):
            g = gh * 2 + jnp.bitwise_xor(core, rel)
            for part in range(0, ROWS, 32):
                images = [x_ref[rel, ih, part : part + 32].astype(F32) for ih in range(4)]
                for b in range(NB):
                    acc_a = jnp.zeros((32, 128), F32)
                    acc_b = jnp.zeros((32, 128), F32)
                    for ih in range(4):
                        at = pl.ds(g * 8 + ih * 2, 1)
                        acc_a = acc_a + images[ih] * fr[b, at, :]
                        acc_b = acc_b + images[ih] * fi[b, at, :]
                    acc = acc_a + pltpu.roll(acc_a, 64, 1)
                    acc_b = acc_b + pltpu.roll(acc_b, 64, 1)
                    first = b * ROWS + part
                    rows[rel, first : first + 32] = (acc + pltpu.roll(acc_b, 32, 1)).astype(BF)
            pos = lists_ref[g, 88:92].astype(jnp.int32)
            sub = lax.broadcasted_iota(jnp.int32, (NV * CAP, 128), 0)
            hot = jnp.concatenate(
                [one_hot(sub, pos[q : q + 1]) for q in range(4)], axis=1
            )
            out = dot16(hot, rows[rel])
            for v in range(NV):
                at = pl.ds(offs_ref[g, v], CAP)
                pool[v, at, :] = pool[v, at, :] + out[v * CAP : (v + 1) * CAP]
    half_rows = (pool.shape[1] - CAP) // 2
    low = lanes((8, half_rows, 128)) < 64
    last = lax.broadcasted_iota(jnp.int32, (8, half_rows, 128), 1) == half_rows - 1
    tight = half_rows == POOL

    def fold(n, carry):
        at = pl.ds(n * 8, 8)
        out = jnp.where(low, pool[at, 0:half_rows], pool[at, half_rows : 2 * half_rows])
        if tight:
            out = jnp.where(last & jnp.logical_not(low), mass.reshape(1, 1, 128), out)
        o_ref[at, 0:half_rows] = out.astype(BF)
        return carry

    lax.fori_loop(0, 8, fold, 0)
    if not tight:
        o_ref[:, half_rows:] = jnp.broadcast_to(mass.reshape(1, 1, 128), (NV, 8, 128)).astype(BF)


def total_kernel(x_ref, f_ref, spread_ref, cols_ref, o_ref, tot, codes):
    tot[...] = jnp.zeros_like(tot)
    columns = cols_ref[...]
    columns = jnp.where(columns < 0, -1, jnp.bitwise_and(columns, 1023))
    codes[...] = slot_rows(columns)
    tight = x_ref.shape[1] == POOL

    def step(nb, carry):
        cols = pltpu.roll(columns, 128 - 4 * nb, 1)
        if tight:
            fill = jnp.zeros((4, 64 - POOL, 128), BF)
            data = jnp.concatenate([x_ref[pl.ds(nb * 4, 4)], fill], axis=1).reshape(256, 128)
        else:
            data = x_ref[pl.ds(nb * 4, 4), 0:64, :].reshape(256, 128)
        kept = []
        for h in range(2):
            col = jnp.concatenate(
                [
                    jnp.broadcast_to(cols[:, 64 * h + v : 64 * h + v + 1], (64, 128))
                    for v in range(4)
                ],
                axis=0,
            )
            k1 = jnp.right_shift(col, 8)
            keep = k1 == lanes((256, 128)) // 32
            wide = dot16(data, spread_ref[h])
            kept.append(
                jnp.concatenate(
                    [jnp.where(keep, wide[:, :128], 0.0), jnp.where(keep, wide[:, 128:], 0.0)],
                    axis=1,
                ).astype(BF)
            )
        kept = jnp.concatenate(
            [kept[h][v * 64 : v * 64 + 64] for v in range(4) for h in range(2)], axis=0
        )
        sub = lax.broadcasted_iota(jnp.int32, (N, 128), 0)
        hot = jnp.concatenate(
            [
                one_hot(sub, jnp.bitwise_and(codes[pl.ds(nb * 4 + v, 1), :], N - 1))
                for v in range(4)
            ],
            axis=1,
        )
        tot[...] += dot16(hot, kept)
        return carry

    lax.fori_loop(0, 16, step, 0, unroll=UNROLL)
    for c in range(2):
        new = (tot[:, c * 128 : c * 128 + 128] + f_ref[c]).astype(BF)
        o_ref[:, c] = new.reshape(NG, FJ, 128)


def mass_kernel(at_ref, sent_ref, cols_ref, o_ref):
    code = slot_rows(cols_ref[...])
    sent = sent_ref[:, 0, :].astype(F32)
    block = jnp.right_shift(code, 10)
    sent = sent + pltpu.roll(sent, 96, 1)
    mass = jnp.take_along_axis(sent, jnp.where(code >= 0, 64 + block, 0), axis=1)
    sub = lax.broadcasted_iota(jnp.int32, (FJ, 128), 0) + at_ref[0] * FJ
    total = [jnp.zeros((FJ, 128), F32) for _ in range(SLAB)]
    for v in range(NV):
        row = code[v : v + 1]
        k1 = jnp.where(row < 0, -1, jnp.bitwise_and(jnp.right_shift(row, 8), 3))
        hot = sub == jnp.bitwise_and(row, N - 1)
        for k in range(SLAB):
            share = jnp.where(k1 == k, mass[v : v + 1], 0.0)
            total[k] = total[k] + jnp.where(hot, share, 0.0)
    lane = lanes((FJ, 128))
    out = jnp.ones((FJ, 128), F32)
    for k in range(SLAB):
        out = jnp.where(lane == k, 1.0 + jnp.sum(total[k], axis=1, keepdims=True), out)
    o_ref[...] = out


def last_kernel(x_ref, m_ref, o_ref):
    scale = 1.0 / m_ref[...]
    for c in range(2):
        for hi in range(2):
            moved = swap4([x_ref[hi * 4 + lo, c].astype(F32) for lo in range(4)])
            for k in range(4):
                o_ref[k, :, c, hi * 128 : hi * 128 + 128] = moved[k] * scale[:, k : k + 1]


def call(kernel, out, name, vmem_bytes=VM, **extra):
    return pl.pallas_call(
        kernel,
        out_shape=out,
        name=name,
        compiler_params=pltpu.CompilerParams(vmem_limit_bytes=vmem_bytes),
        **extra,
    )


def struct(shape, dtype=F32):
    return jax.ShapeDtypeStruct(shape, dtype)


def over_img(x):
    return lax.all_to_all(x, "img", split_axis=0, concat_axis=0, tiled=True)


def over_vol(x):
    return lax.all_to_all(x, "vol", split_axis=0, concat_axis=0, tiled=True)


def phase_tables():
    freq = np.arange(N).reshape(NG, FJ)
    shift = np.arange(32) - 8
    ang = 2.0 * np.pi * ((freq[:, :, None] * shift[None, None, :]) % N) / N
    cos_t, sin_t = np.cos(ang), np.sin(ang)
    score = np.zeros((NG, 2, 2, 2, FJ, 2, NB, 32), np.float32)
    back = np.zeros((NG, NB, 32, 2, 2, 2, FJ), np.float32)
    for c in range(2):
        sign = 1.0 if c else -1.0
        for lo in range(2):
            score[:, 0, lo, c, :, lo] = cos_t[:, :, None, :]
            score[:, 1, lo, c, :, lo] = sign * sin_t[:, :, None, :]
            back[:, :, :, 0, lo, c, :] = cos_t.transpose(0, 2, 1)[:, None]
            back[:, :, :, 1, lo, c, :] = sign * sin_t.transpose(0, 2, 1)[:, None]
    return score.reshape(NG, 2, 128, 256), back.reshape(NG, 128, 256)


def pipeline(half_rows, density, images, block_tiles, image_blocks, shifts, precision):
    vol_at = lax.axis_index("vol")
    img_at = lax.axis_index("img")
    score_t, back_t = phase_tables()
    score_t = lax.dynamic_slice_in_dim(jnp.asarray(score_t), img_at, 1, 0)
    back_t = lax.dynamic_slice_in_dim(jnp.asarray(back_t), img_at, 1, 0)
    smem = pl.BlockSpec(memory_space=pltpu.SMEM)
    vmem = pl.BlockSpec(memory_space=pltpu.VMEM)
    hbm = pl.BlockSpec(memory_space=pltpu.HBM)

    one = call(
        first_kernel,
        struct((NG, 120, 128)),
        "third_index",
        vmem_bytes=63 * 1000 * 1000,
        in_specs=[smem] + [hbm] * 6,
        scratch_shapes=[
            pltpu.VMEM((4, FJ, N), F32),
            pltpu.VMEM((N, 2 * N), F32),
            pltpu.VMEM((NV * NB, ROWS), jnp.int32),
            pltpu.VMEM((2, NG), jnp.int32),
            pltpu.VMEM((NG, TR), jnp.int32),
            pltpu.VMEM((1, NG), F32),
            pltpu.SemaphoreType.DMA((6,)),
        ],
    )(
        vol_at.reshape(1).astype(jnp.int32),
        density,
        table_first(),
        block_tiles,
        image_blocks.T,
        shifts,
        precision.reshape(1, NG),
    )
    images, one = lax.optimization_barrier((images, one))
    lists = over_img(one)

    own_at = img_at.reshape(1).astype(jnp.int32)
    own, other = call(
        image_kernel,
        (struct((4, 4, ROWS, 128), BF),) * 2,
        "image_split",
        grid=(4,),
        in_specs=[smem, pl.BlockSpec((2, 2, ROWS, N), lambda i: (i, 0, 0, 0))],
        out_specs=(pl.BlockSpec((4, 1, ROWS, 128), lambda i: (0, i, 0, 0)),) * 2,
    )(own_at, images)
    lists, own, other = lax.optimization_barrier((lists, own, other))
    two = call(second_kernel, struct((NV, 8, 128)), "second_index")(lists, table_second())
    two, other = lax.optimization_barrier((two, other))
    sibling = lax.ppermute(other, "img", [(i, i ^ 1) for i in range(NG)])
    cols, offs, flag, third = call(
        pool_kernel,
        (
            struct((2, 64, 128), jnp.int32),
            struct((2, NG, 128), jnp.int32),
            struct((8, 128), jnp.int32),
            struct((2, N, N)),
        ),
        "pools",
    )(lists, table_third())
    pairs = jnp.stack([own, sibling], axis=1)
    two = over_vol(two)
    two, pairs = lax.optimization_barrier((two, pairs))

    done = exchange(half_rows, own_at, two, pairs, lists, cols, offs, third, score_t, back_t)
    return done, flag


def per_device(*inputs):
    done, flag = pipeline(POOL, *inputs)
    updated, posterior = lax.cond(
        flag[0, 0] > 0,
        lambda done, *rest: done,
        lambda done, *rest: pipeline(64, *rest)[0],
        done,
        *inputs,
    )
    return (updated, posterior)


def exchange(rows, own_at, two, pairs, lists, cols, offs, third, score_t, back_t):
    smem = pl.BlockSpec(memory_space=pltpu.SMEM)
    vmem = pl.BlockSpec(memory_space=pltpu.VMEM)
    hbm = pl.BlockSpec(memory_space=pltpu.HBM)
    tight = rows == POOL
    cols = cols[0 if tight else 1]
    offs = offs[0 if tight else 1]
    fourier, outgoing = call(
        gather_kernel,
        (struct((2, N, 128)), struct((NV, rows, 128), BF)),
        "slice_tiles",
        in_specs=[vmem] * 4,
        out_specs=(vmem, hbm),
        scratch_shapes=[
            pltpu.VMEM((N, N), BF),
            pltpu.VMEM((NV, rows, 128), BF),
            pltpu.SemaphoreType.DMA((16,)),
        ],
    )(two, third, jnp.asarray(table_fold(), BF), cols)
    outgoing, pairs = lax.optimization_barrier((outgoing, pairs))
    incoming = over_vol(outgoing)
    from_chip = [pairs[0]] + [
        lax.ppermute(pairs[d], "img", [(i, (i + 2 * d) % NG) for i in range(NG)])
        for d in range(1, 4)
    ]
    partial = call(
        score_kernel,
        struct((NG, 16, 128)),
        "score",
        in_specs=[smem] * 2 + [vmem] * 7,
        scratch_shapes=[pltpu.VMEM((NB, 64, 128), F32)] * 3
        + [pltpu.VMEM((NV, 2 * rows + CAP, 128), F32), pltpu.VMEM((NV * CAP, 128), BF)],
    )(own_at, offs, *from_chip, incoming, lists, score_t)
    partial = over_img(partial)

    weights, back = call(
        back_kernel,
        (struct((64, 128)), struct((NV, rows if tight else rows + 8, 128), BF)),
        "backproject",
        in_specs=[smem] * 2 + [vmem] * 7,
        scratch_shapes=[
            pltpu.VMEM((NB, 64, 128), F32),
            pltpu.VMEM((NB, 64, 128), F32),
            pltpu.VMEM((2, 512, 128), BF),
            pltpu.VMEM((NV, 2 * rows + CAP, 128), F32),
        ],
    )(own_at, offs, *from_chip, partial, lists, back_t)
    returned = over_vol(back)

    updated = call(
        total_kernel,
        struct((NG, 2, FJ, 128), BF),
        "totals",
        scratch_shapes=[pltpu.VMEM((N, N), F32), pltpu.VMEM((NV, 128), jnp.int32)],
    )(returned, fourier, jnp.asarray(table_spread(), BF), cols)
    at = rows - 1 if tight else rows
    sent = jnp.broadcast_to(lax.slice_in_dim(returned, at, at + 1, axis=1), (NV, 8, 128))
    sent, updated = lax.optimization_barrier((sent, updated))
    updated = over_img(updated)
    masses = call(
        mass_kernel, struct((FJ, 128)), "masses", in_specs=[smem, vmem, vmem]
    )(own_at, sent, cols)
    updated = call(last_kernel, struct((SLAB, FJ, 2, N)), "frequency_join")(updated, masses)
    weights = lax.dynamic_slice_in_dim(weights, own_at[0] * 8, 8, 0)[:, : 2 * TR]
    return lax.optimization_barrier((updated, weights.reshape(NG, 2, TR)))


def solution(mesh):
    in_specs = (
        P("vol", "img", None),
        P(("img", "vol"), None, None, None),
        P("img", None),
        P(("img", "vol"), None),
        P(("img", "vol"), None),
        P(("img", "vol")),
    )
    out_specs = (P("vol", "img", None, None), P(("img", "vol"), None, None))
    return jax.shard_map(
        per_device, mesh=mesh, in_specs=in_specs, out_specs=out_specs, check_vma=False
    )
```
